32 devices in a mesh: gx: 8 (over z, x), gy: 2 (over y), gz: 2 (over core).
Axes of the slice: x: 2, y: 2, z: 4, core: 2. Of those that a mesh axis runs over, the one named last changes fastest.
Arguments:
- velocity: float32 [3, 32, 64, 1024], P(None, 'gz', 'gx', 'gy'), may hold values from -6 to 6
- column_state: float32 [2, 64, 64, 1024], P(None, None, 'gx', ('gy', 'gz')), may hold values from -4 to 4
- height_index: int32 [64, 1024], P('gx', 'gy'), may hold values from 1 to 8
- rotor_mask: int32 [32, 64, 1024], P('gz', 'gx', 'gy'), may hold values from 0 to 8, as said below
- thrust: float32 [8], replicated, may hold values from 1 to 4
Outputs:
- advanced: float32 [3, 32, 64, 1024], P(None, 'gz', 'gx', 'gy')
- fresh_state: float32 [2, 64, 64, 1024], P(None, None, 'gx', ('gy', 'gz'))
The draws below stay inside these ranges and needn't reach their ends.
Inputs may be any that keep to these rules, and one draw needn't show every extreme that they name: `height_index`: each ground face's sampling layer, counted from the ground. `rotor_mask`: cells holding k + 1 form rotor k's disk of radius 6 cells; all 8 disks lie in one z layer between 2 and 9.
All inputs are finite; a program needn't handle non-finite values.
Results may differ from the reference program's by a relative error of at most 0.000034.
Values sent between devices are 32-bit elements; how exact they have to be, the bound alone decides.
A program may use at most 64 MiB of HBM per device.

```python
import math
import jax
import jax.numpy as jnp
from jax import lax

POINTS = 64
LEVELS = 8
ROTORS = 8
NX = 64
NY = 1024
NZ = 32
N_GY = 2
N_GZ = 2


disk_radius = 6


cycle_offsets = [(18, 0), (13, 13), (0, 18), (-13, 13), (-18, 0), (-13, -13), (0, -18), (13, -13)]


def draw_rotor_mask(key, part):
    key = jax.random.fold_in(key, 7)
    keys = jax.random.split(key, 3)
    centre_x = jax.random.randint(keys[0], (), 0, NX)
    centre_y = jax.random.randint(keys[1], (), 0, NY)
    hover_layer = jax.random.randint(keys[2], (), 2, 10)
    x_cells = jnp.arange(NX, dtype=jnp.int32)[:, None]
    y_cells = jnp.arange(NY, dtype=jnp.int32)[None, :]
    plane = jnp.zeros((NX, NY), jnp.int32)
    for rotor_id in range(len(cycle_offsets)):
        offset_x, offset_y = cycle_offsets[rotor_id]
        dist_x = (x_cells - centre_x - offset_x) % NX
        dist_x = jnp.minimum(dist_x, NX - dist_x)
        dist_y = (y_cells - centre_y - offset_y) % NY
        dist_y = jnp.minimum(dist_y, NY - dist_y)
        inside = dist_x * dist_x + dist_y * dist_y <= disk_radius * disk_radius
        plane = jnp.where(inside, jnp.maximum(plane, rotor_id + 1), plane)
    z_cells = jnp.arange(NZ, dtype=jnp.int32)[:, None, None]
    return jnp.where(z_cells == hover_layer, plane[None], 0).astype(jnp.int32)


def with_ends(array, key, least, top_value):
    longest = array.shape.index(max(array.shape))
    spots = []
    for shift in (0, 1):
        where = [jax.random.randint(jax.random.fold_in(key, axis), (), 0, length) for axis, length in enumerate(array.shape)]
        where[longest] = (where[longest] + shift) % array.shape[longest]
        spots.append(tuple(where))
    return array.at[spots[0]].set(least).at[spots[1]].set(top_value)


def level_of(own_key, dims, cuts, low, largest):
    def one(dim, blocks):
        steps = jax.random.uniform(jax.random.fold_in(jax.random.fold_in(own_key, 6), dim), (blocks,), jnp.float32, low / len(cuts), largest / len(cuts))
        return jnp.repeat(jnp.exp(steps), dims[dim] // blocks).reshape((-1,) + (1,) * (len(dims) - dim - 1))

    gain = one(*cuts[0])
    for cut in cuts[1:]:
        gain = gain * one(*cut)
    return gain


def normal_values(own_key, dims, width, bound, cuts=(), held_as=jnp.bfloat16):
    array = width * jax.random.normal(own_key, dims, jnp.float32)
    if cuts:
        array = array * level_of(own_key, dims, cuts, -0.22, 0.18)
    return jnp.clip(array, -bound, bound).astype(held_as)


def setup_inputs(seed: int = 0) -> dict:
    key_of = jax.random.split(jax.random.key(seed), 6)
    return {
        "velocity": normal_values(key_of[0], (3, NZ, NX, NY), 1.0, 6.0, ((1, 2), (2, 8), (3, 2)), jnp.float32),
        "column_state": normal_values(key_of[1], (2, POINTS, NX, NY), 0.5, 4.0, ((2, 8), (3, 4)), jnp.float32),
        "height_index": with_ends(jax.random.randint(key_of[2], (NX, NY), 1, LEVELS + 1), jax.random.fold_in(key_of[2], 1), 1, LEVELS).astype(jnp.int32),
        "rotor_mask": draw_rotor_mask(jax.random.fold_in(key_of[5], 71), 0),
        "thrust": jnp.clip(jnp.exp(jax.random.uniform(key_of[4], (ROTORS,), jnp.float32, math.log(1.0), math.log(4.0))), 1.0, 4.0),
    }


time_step = 0.1
viscosity = 0.02
smag_coeff = 0.0289
karman = 0.41
wall_step = 0.05
stretch = 3.0

def sample(lowest, height_index):
    picked = jnp.zeros_like(lowest[:, 0])
    for layer_z in range(1, lowest.shape[1]):
        picked = picked + jnp.where((height_index == layer_z)[None], lowest[:, layer_z], 0.0)
    return picked

def column_step(state, top_speed, sample_height):
    count = state.shape[1]
    ladder = jnp.arange(count, dtype=jnp.float32) / (count - 1)
    spacing = (jnp.exp(stretch * ladder) - 1.0) / (math.exp(stretch) - 1.0)
    heights = spacing.reshape((count,) + (1,) * sample_height.ndim) * sample_height[None]
    spacing_gap = heights[1:] - heights[:-1]
    middle = 0.5 * (heights[1:] + heights[:-1])
    differ = state[:, 1:] - state[:, :-1]
    shear_rate = jnp.sqrt(differ[0] * differ[0] + differ[1] * differ[1] + 1e-06) / spacing_gap
    eddy_visc = viscosity + (karman * middle) ** 2 * shear_rate
    conduct = eddy_visc / spacing_gap
    volume = 0.5 * (spacing_gap[1:] + spacing_gap[:-1]) / wall_step
    band_low = -conduct[:-1]
    band_up = -conduct[1:]
    band_mid = volume + conduct[:-1] + conduct[1:]
    source = volume[None] * state[:, 1:-1]
    source = source.at[:, -1].add(conduct[-1][None] * top_speed)

    def forward(pair_in, entries):
        prev_c, prev_d = pair_in
        low_e, mid_e, up_e, src_e = entries
        denom = mid_e - low_e * prev_c
        cur_c = up_e / denom
        cur_d = (src_e - low_e[None] * prev_d) / denom[None]
        return ((cur_c, cur_d), (cur_c, cur_d))
    start_pair = (jnp.zeros_like(sample_height), jnp.zeros_like(top_speed))
    _, (coef_c, coef_d) = lax.scan(forward, start_pair, (band_low, band_mid, band_up, jnp.moveaxis(source, 1, 0)), unroll=True)

    def backward(later, entries):
        cur_c, cur_d = entries
        value = cur_d - cur_c[None] * later
        return (value, value)
    _, solved = lax.scan(backward, jnp.zeros_like(top_speed), (coef_c, coef_d), reverse=True, unroll=True)
    solved = jnp.moveaxis(solved, 0, 1)
    fresh = jnp.concatenate([jnp.zeros_like(solved[:, :1]), solved, top_speed[:, None]], axis=1)
    stress = conduct[0][None] * solved[:, 0]
    return (fresh, stress)

def advance(velocity, planar, stacked, stress, bottom_flag, rotor_mask, thrust):
    x_next = planar[:, :, 2:, 1:-1]
    x_prev = planar[:, :, :-2, 1:-1]
    y_next = planar[:, :, 1:-1, 2:]
    y_prev = planar[:, :, 1:-1, :-2]
    z_next = stacked[:, 2:]
    z_prev = stacked[:, :-2]
    grad_x = 0.5 * (x_next - x_prev)
    grad_y = 0.5 * (y_next - y_prev)
    grad_z = 0.5 * (z_next - z_prev)
    strain_xy = 0.5 * (grad_y[0] + grad_x[1])
    strain_xz = 0.5 * (grad_z[0] + grad_x[2])
    strain_yz = 0.5 * (grad_z[1] + grad_y[2])
    diag_part = grad_x[0] * grad_x[0] + grad_y[1] * grad_y[1] + grad_z[2] * grad_z[2]
    cross_part = strain_xy * strain_xy + strain_xz * strain_xz + strain_yz * strain_yz
    strain_norm = jnp.sqrt(2.0 * diag_part + 4.0 * cross_part + 1e-06)
    viscous = viscosity + smag_coeff * strain_norm
    laplace = x_next + x_prev + y_next + y_prev + z_next + z_prev - 6.0 * velocity
    advect = 0.5 * (x_next * x_next[0:1] - x_prev * x_prev[0:1])
    advect = advect + 0.5 * (y_next * y_next[1:2] - y_prev * y_prev[1:2])
    advect = advect + 0.5 * (z_next * z_next[2:3] - z_prev * z_prev[2:3])
    tendency = viscous[None] * laplace - advect
    wall_term = viscous[0][None] * velocity[:2, 0] - stress
    tendency = tendency.at[:2, 0].add(bottom_flag * wall_term)
    thrust_force = jnp.zeros_like(velocity[2])
    for rotor_id in range(thrust.shape[0]):
        thrust_force = thrust_force + jnp.where(rotor_mask == rotor_id + 1, thrust[rotor_id], 0.0)
    tendency = tendency.at[2].add(-thrust_force)
    return velocity + time_step * tendency

def to_columns(ground):
    lead_dims = ground.shape[:-1]
    groups = N_GY * N_GZ
    block_len = NY // (N_GY * groups)
    blocks_view = ground.reshape(lead_dims + (N_GY, groups, block_len))
    return jnp.moveaxis(blocks_view, -3, -1).reshape(lead_dims + (NY,))

def to_ground(columns_in):
    lead_dims = columns_in.shape[:-1]
    groups = N_GY * N_GZ
    block_len = NY // (N_GY * groups)
    blocks_view = columns_in.reshape(lead_dims + (groups, block_len, N_GY))
    return jnp.moveaxis(blocks_view, -1, -3).reshape(lead_dims + (NY,))

def reference(velocity, column_state, height_index, rotor_mask, thrust):
    top_speed = sample(velocity[:2, :LEVELS + 1], height_index)
    sample_height = height_index.astype(jnp.float32) + 0.5
    fresh_state, stress_cols = column_step(column_state, to_columns(top_speed), to_columns(sample_height))
    stress = to_ground(stress_cols)
    planar = jnp.pad(velocity, ((0, 0), (0, 0), (1, 1), (1, 1)), mode='wrap')
    stacked = jnp.pad(velocity, ((0, 0), (1, 1), (0, 0), (0, 0)))
    advanced = advance(velocity, planar, stacked, stress, 1.0, rotor_mask, thrust)
    return (advanced, fresh_state)
```

```python
import functools
import math

import jax
import jax.numpy as jnp
import numpy as np
from jax import lax
from jax.experimental import pallas as pl
from jax.experimental.pallas import tpu as pltpu
from jax.sharding import PartitionSpec as P

LEVELS = 8
LANES = 128
MESH = pl.DeviceIdType.MESH
CHUNKS = 4

time_step = 0.1
viscosity = 0.02
smag_coeff = 0.0289
karman = 0.41
wall_step = 0.05
stretch = 3.0


def column_constants(points):
    ladder = np.arange(points, dtype=np.float64) / (points - 1)
    spacing = (np.exp(stretch * ladder) - 1.0) / (math.exp(stretch) - 1.0)
    gap = spacing[1:] - spacing[:-1]
    middle = 0.5 * (spacing[1:] + spacing[:-1])
    laminar = viscosity / gap
    eddy = (karman * middle / gap) ** 2
    volume = np.zeros_like(gap)
    volume[1:] = 0.5 * (gap[1:] + gap[:-1]) / wall_step
    return [[float(np.float32(v)) for v in row] for row in (laminar, eddy, volume)]


def kernel(
    sizes,
    v_hbm, s_hbm, h_hbm, m_hbm, thrust_ref, tab_ref,
    adv_ref, fresh_ref,
    v, s, h, mask, eddy, coef_e, coef_f,
    xlo, xhi, zhalo, ypack_lo, ypack_hi, ylo, yhi,
    stage, tops, back, walls, plane,
    load_sem, x_send, x_recv, y_send, y_recv, z_send, z_recv, t_send, t_recv, w_send, w_recv,
):
    n_gx, n_gy, n_gz, layers, rows, width, points, cols = sizes
    group = n_gy * n_gz
    block = width // group
    tiles = width // LANES
    gx, gy, gz = lax.axis_index("gx"), lax.axis_index("gy"), lax.axis_index("gz")
    me = gy * n_gz + gz
    left, right = lax.rem(gx + n_gx - 1, n_gx), lax.rem(gx + 1, n_gx)
    below, above = lax.rem(gy + n_gy - 1, n_gy), lax.rem(gy + 1, n_gy)
    at_wall = gz == 0

    loads = [
        pltpu.make_async_copy(h_hbm, h, load_sem.at[0]),
        pltpu.make_async_copy(
            v_hbm.at[pl.ds(0, 2), pl.ds(0, LEVELS + 1)], v.at[pl.ds(0, 2), pl.ds(0, LEVELS + 1)], load_sem.at[1]
        ),
        pltpu.make_async_copy(
            v_hbm.at[pl.ds(0, 2), pl.ds(LEVELS + 1, layers - LEVELS - 1)],
            v.at[pl.ds(0, 2), pl.ds(LEVELS + 1, layers - LEVELS - 1)],
            load_sem.at[2],
        ),
        pltpu.make_async_copy(v_hbm.at[2], v.at[2], load_sem.at[3]),
        pltpu.make_async_copy(s_hbm, s, load_sem.at[4]),
        pltpu.make_async_copy(m_hbm.at[pl.ds(2, 8)], mask, load_sem.at[5]),
    ]
    for load in loads:
        load.start()

    barrier = pltpu.get_barrier_semaphore()
    for side in (left, right):
        pl.semaphore_signal(barrier, inc=1, device_id=(side, gy, gz), device_id_type=MESH)
    for d in range(1, group):
        r = lax.rem(me + d, group)
        pl.semaphore_signal(barrier, inc=1, device_id=(gx, r // n_gz, r % n_gz), device_id_type=MESH)

    loads[0].wait()
    loads[1].wait()

    @pl.when(at_wall)
    def _():
        height = h[...]
        for c in range(2):
            picked = v[c, LEVELS]
            for level in range(1, LEVELS):
                picked = jnp.where(height == level, v[c, level], picked)
            for r in range(group):
                j, off = (r * block) // LANES, (r * block) % LANES
                part = picked[:, j * LANES : (j + 1) * LANES]
                if off:
                    part = pltpu.roll(part, LANES - off, 1)
                stage[r, c] = part
        sample_height = height.astype(jnp.float32) + 0.5
        for r in range(group):
            j, off = (r * block) // LANES, (r * block) % LANES
            part = sample_height[:, j * LANES : (j + 1) * LANES]
            if off:
                part = pltpu.roll(part, LANES - off, 1)
            stage[r, 2] = part
        tops[gy] = stage[me]

    pl.semaphore_wait(barrier, 2 + group - 1)

    def top_send(d):
        r = lax.rem(me + d, group)
        return pltpu.make_async_remote_copy(
            src_ref=stage.at[r], dst_ref=tops.at[gy], send_sem=t_send.at[d], recv_sem=t_recv.at[gy],
            device_id=(gx, r // n_gz, r % n_gz), device_id_type=MESH,
        )

    @pl.when(at_wall)
    def _():
        for d in range(1, group):
            top_send(d).start()

    def x_copies(k):
        depth = layers // CHUNKS
        zs = pl.ds((CHUNKS - 1 - k) * depth, depth)
        to_right = pltpu.make_async_remote_copy(
            src_ref=v_hbm.at[:, zs, pl.ds(rows - 1, 1)], dst_ref=xlo.at[:, zs],
            send_sem=x_send.at[2 * k], recv_sem=x_recv.at[2 * k],
            device_id=(right, gy, gz), device_id_type=MESH,
        )
        to_left = pltpu.make_async_remote_copy(
            src_ref=v_hbm.at[:, zs, pl.ds(0, 1)], dst_ref=xhi.at[:, zs],
            send_sem=x_send.at[2 * k + 1], recv_sem=x_recv.at[2 * k + 1],
            device_id=(left, gy, gz), device_id_type=MESH,
        )
        return to_right, to_left

    for k in range(CHUNKS):
        for copy in x_copies(k):
            copy.start()

    edge = (layers - 1) * (1 - gz)
    z_copy = pltpu.make_async_remote_copy(
        src_ref=v_hbm.at[:, edge], dst_ref=zhalo, send_sem=z_send.at[0], recv_sem=z_recv.at[0],
        device_id=(gx, gy, 1 - gz), device_id_type=MESH,
    )
    z_copy.start()

    loads[2].wait()
    loads[3].wait()
    lane = lax.broadcasted_iota(jnp.int32, (rows, LANES), 1)

    def pack(k, carry):
        low, high = carry
        c, z = k // layers, k % layers
        low = jnp.where(lane == k, pltpu.roll(v[c, z, :, :LANES], k, 1), low)
        high = jnp.where(lane == k, pltpu.roll(v[c, z, :, width - LANES :], k + 1, 1), high)
        return low, high

    zeros = jnp.zeros((rows, LANES), jnp.float32)
    low, high = lax.fori_loop(0, 3 * layers, pack, (zeros, zeros), unroll=4)
    ypack_lo[...] = low
    ypack_hi[...] = high
    y_copies = [
        pltpu.make_async_remote_copy(
            src_ref=ypack_hi, dst_ref=ylo, send_sem=y_send.at[0], recv_sem=y_recv.at[0],
            device_id=(gx, above, gz), device_id_type=MESH,
        ),
        pltpu.make_async_remote_copy(
            src_ref=ypack_lo, dst_ref=yhi, send_sem=y_send.at[1], recv_sem=y_recv.at[1],
            device_id=(gx, below, gz), device_id_type=MESH,
        ),
    ]
    for copy in y_copies:
        copy.start()

    loads[4].wait()

    def shear(i, carry):
        du = s[0, i + 1] - s[0, i]
        dv = s[1, i + 1] - s[1, i]
        eddy[i] = tab_ref[1, i] * jnp.sqrt(du * du + dv * dv + 1e-06)
        return carry

    lax.fori_loop(0, points - 1, shear, 0, unroll=3)

    def top_wait(src):
        pltpu.make_async_remote_copy(
            src_ref=stage.at[0], dst_ref=tops.at[src], send_sem=t_send.at[0], recv_sem=t_recv.at[src],
            device_id=(gx, gy, 1 - gz), device_id_type=MESH,
        ).wait_recv()

    for src in range(n_gy):

        @pl.when(me != src * n_gz)
        def _():
            top_wait(src)

    lane_wide = lax.broadcasted_iota(jnp.int32, (rows, cols), 1)
    halves = cols // LANES

    def interleave(field):
        parts = []
        for half in range(halves):
            source = (lane + half * LANES) // n_gy
            owner = (lane + half * LANES) % n_gy
            out = None
            for src in range(n_gy):
                got = jnp.take_along_axis(tops[src, field], source, axis=1, mode="promise_in_bounds")
                out = got if out is None else jnp.where(owner == src, got, out)
            parts.append(out)
        return jnp.concatenate(parts, axis=1)

    top_u, top_v, height = interleave(0), interleave(1), interleave(2)
    inv_height = 1.0 / height

    last = points - 1
    fresh_ref[0, last] = top_u
    fresh_ref[1, last] = top_v
    fresh_ref[0, 0] = jnp.zeros_like(top_u)
    fresh_ref[1, 0] = jnp.zeros_like(top_u)

    def eliminate(k, carry):
        share, cond, f_u, f_v = carry
        i = last - 1 - k
        cond_low = tab_ref[0, i - 1] * inv_height + eddy[i - 1]
        volume = tab_ref[2, i] * height
        held = volume + share
        inverse = 1.0 / (held + cond_low)
        f_u = (volume * s[0, i] + cond * f_u) * inverse
        f_v = (volume * s[1, i] + cond * f_v) * inverse
        coef_e[i] = cond_low * inverse
        coef_f[0, i] = f_u
        coef_f[1, i] = f_v
        return cond_low * (held * inverse), cond_low, f_u, f_v

    cond_top = tab_ref[0, last - 1] * inv_height + eddy[last - 1]
    _, cond, f_u, f_v = lax.fori_loop(0, points - 2, eliminate, (cond_top, cond_top, top_u, top_v), unroll=2)
    stress = (cond * f_u, cond * f_v)

    for src in range(n_gy):
        index = lane * n_gy + src
        index = jnp.where(index < cols, index, 0)
        for c in range(2):
            out = None
            for half in range(halves):
                got = jnp.take_along_axis(
                    stress[c][:, half * LANES : (half + 1) * LANES], index % LANES, axis=1, mode="promise_in_bounds"
                )
                out = got if out is None else jnp.where(index // LANES == half, got, out)
            back[src, c] = out

    def wall_send(src):
        return pltpu.make_async_remote_copy(
            src_ref=back.at[src], dst_ref=walls.at[me], send_sem=w_send.at[src], recv_sem=w_recv.at[me],
            device_id=(gx, src, 0), device_id_type=MESH,
        )

    for src in range(n_gy):

        @pl.when(me != src * n_gz)
        def _():
            wall_send(src).start()

    @pl.when(at_wall)
    def _():
        walls[me] = back[gy]

    def substitute(k, carry):
        u, w = carry
        i = k + 1
        e = coef_e[i]
        u = e * u + coef_f[0, i]
        w = e * w + coef_f[1, i]
        fresh_ref[0, i] = u
        fresh_ref[1, i] = w
        return u, w

    zero = jnp.zeros_like(top_u)
    lax.fori_loop(0, points - 2, substitute, (zero, zero), unroll=2)

    for copy in y_copies:
        copy.wait_recv()
    z_copy.wait_recv()
    loads[5].wait()

    disks = mask[0]
    for k in range(1, 8):
        disks = jnp.maximum(disks, mask[k])
    force = jnp.zeros((rows, width), jnp.float32)
    for k in range(8):
        force = force + jnp.where(disks == k + 1, thrust_ref[k], 0.0)
    plane[...] = force * time_step

    row = lax.broadcasted_iota(jnp.int32, (rows, width), 0)
    col = lax.broadcasted_iota(jnp.int32, (rows, width), 1)

    def layer(z, below_v, above_v, wall):
        vel, xn, xp, yn, yp = [], [], [], [], []
        for c in range(3):
            here = v[c, z]
            vel.append(here)
            xp.append(jnp.where(row == 0, xlo[c, z], pltpu.roll(here, 1, 0)))
            xn.append(jnp.where(row == rows - 1, xhi[c, z], pltpu.roll(here, rows - 1, 0)))
            slot = c * layers + z
            low = pltpu.roll(ylo[...], LANES - slot, 1)
            high = pltpu.roll(yhi[...], LANES - 1 - slot, 1)
            low = jnp.concatenate([low] * tiles, axis=1)
            high = jnp.concatenate([high] * tiles, axis=1)
            yp.append(jnp.where(col == 0, low, pltpu.roll(here, 1, 1)))
            yn.append(jnp.where(col == width - 1, high, pltpu.roll(here, width - 1, 1)))
        zn, zp = above_v, below_v
        d_x = [xn[c] - xp[c] for c in range(3)]
        d_y = [yn[c] - yp[c] for c in range(3)]
        d_z = [zn[c] - zp[c] for c in range(3)]
        diag = d_x[0] * d_x[0] + d_y[1] * d_y[1] + d_z[2] * d_z[2]
        s_xy, s_xz, s_yz = d_y[0] + d_x[1], d_z[0] + d_x[2], d_z[1] + d_y[2]
        cross = s_xy * s_xy + s_xz * s_xz + s_yz * s_yz
        strain = jnp.sqrt(0.5 * diag + (0.25 * cross + 1e-06))
        viscous = time_step * viscosity + (time_step * smag_coeff) * strain
        for c in range(3):
            total = (xn[c] + xp[c]) + (yn[c] + yp[c]) + (zn[c] + zp[c])
            flux = (
                (xn[c] * xn[0] - xp[c] * xp[0]) + (yn[c] * yn[1] - yp[c] * yp[1]) + (zn[c] * zn[2] - zp[c] * zp[2])
            )
            lap = total - 6.0 * vel[c]
            if wall is not None and c < 2:
                lap = lap + wall[0] * vel[c]
            out = vel[c] + (viscous * lap - (0.5 * time_step) * flux)
            if wall is not None and c < 2:
                out = out - time_step * wall[1][c]
            adv_ref[c, z] = out

    def velocity_at(z):
        return [v[c, z] for c in range(3)]

    def x_wait(k):
        for copy in x_copies(k):
            copy.wait_recv()

    depth = layers // CHUNKS
    x_wait(0)
    bottom = at_wall.astype(jnp.float32)
    layer(layers - 1, velocity_at(layers - 2), [zhalo[c] * bottom for c in range(3)], None)

    def inner(z, carry):
        layer(z, velocity_at(z - 1), velocity_at(z + 1), None)
        return carry

    lax.fori_loop(layers - depth, layers - 1, inner, 0)
    for k in range(1, CHUNKS):
        x_wait(k)
        low = (CHUNKS - 1 - k) * depth
        lax.fori_loop(max(low, 1), low + depth, inner, 0)

    def wall_wait(r):
        pltpu.make_async_remote_copy(
            src_ref=back.at[0], dst_ref=walls.at[r], send_sem=w_send.at[0], recv_sem=w_recv.at[r],
            device_id=(gx, gy, 1 - gz), device_id_type=MESH,
        ).wait_recv()

    @pl.when(at_wall)
    def _():
        for r in range(group):

            @pl.when(me != r)
            def _():
                wall_wait(r)

        wall = []
        for c in range(2):
            parts = []
            for j in range(tiles):
                out = None
                for r in range(group):
                    if (r * block) // LANES == j:
                        off = (r * block) % LANES
                        got = walls[r, c]
                        if off:
                            got = pltpu.roll(got, off, 1)
                        out = got if out is None else jnp.where(lane >= off, got, out)
                parts.append(out)
            wall.append(jnp.concatenate(parts, axis=1))
        layer(0, [jnp.zeros((rows, width), jnp.float32)] * 3, velocity_at(1), (1.0, wall))

        for k in range(8):
            adv_ref[2, 2 + k] = adv_ref[2, 2 + k] - jnp.where(mask[k] != 0, plane[...], 0.0)

    @pl.when(jnp.logical_not(at_wall))
    def _():
        layer(0, [zhalo[c] for c in range(3)], velocity_at(1), None)

    @pl.when(at_wall)
    def _():
        for d in range(1, group):
            top_send(d).wait_send()

    for src in range(n_gy):

        @pl.when(me != src * n_gz)
        def _():
            wall_send(src).wait_send()

    for k in range(CHUNKS):
        for copy in x_copies(k):
            copy.wait_send()
    for copy in y_copies:
        copy.wait_send()
    z_copy.wait_send()


def local(n_gx, n_gy, n_gz, velocity, column_state, height_index, rotor_mask, thrust):
    _, layers, rows, width = velocity.shape
    _, points, _, cols = column_state.shape
    group = n_gy * n_gz
    table = jnp.asarray(np.asarray(column_constants(points), np.float32))
    any_spec = pl.BlockSpec(memory_space=pl.ANY)
    smem_spec = pl.BlockSpec(memory_space=pltpu.SMEM)
    vmem_spec = pl.BlockSpec(memory_space=pltpu.VMEM)
    f32 = jnp.float32
    dma = pltpu.SemaphoreType.DMA
    scratch = [
        pltpu.VMEM(velocity.shape, f32),
        pltpu.VMEM(column_state.shape, f32),
        pltpu.VMEM(height_index.shape, jnp.int32),
        pltpu.VMEM((8, rows, width), jnp.int32),
        pltpu.VMEM((points - 1, rows, cols), f32),
        pltpu.VMEM((points - 1, rows, cols), f32),
        pltpu.VMEM((2, points - 1, rows, cols), f32),
        pltpu.VMEM((3, layers, 1, width), f32),
        pltpu.VMEM((3, layers, 1, width), f32),
        pltpu.VMEM((3, rows, width), f32),
        pltpu.VMEM((rows, LANES), f32),
        pltpu.VMEM((rows, LANES), f32),
        pltpu.VMEM((rows, LANES), f32),
        pltpu.VMEM((rows, LANES), f32),
        pltpu.VMEM((group, 3, rows, LANES), f32),
        pltpu.VMEM((n_gy, 3, rows, LANES), f32),
        pltpu.VMEM((n_gy, 2, rows, LANES), f32),
        pltpu.VMEM((group, 2, rows, LANES), f32),
        pltpu.VMEM((rows, width), f32),
        dma((6,)),
        dma((2 * CHUNKS,)), dma((2 * CHUNKS,)),
        dma((2,)), dma((2,)),
        dma((1,)), dma((1,)),
        dma((group,)), dma((n_gy,)),
        dma((n_gy,)), dma((group,)),
    ]
    sizes = (n_gx, n_gy, n_gz, layers, rows, width, points, cols)
    return pl.pallas_call(
        functools.partial(kernel, sizes),
        out_shape=(
            jax.ShapeDtypeStruct(velocity.shape, f32),
            jax.ShapeDtypeStruct(column_state.shape, f32),
        ),
        in_specs=[any_spec] * 4 + [smem_spec] * 2,
        out_specs=(vmem_spec, vmem_spec),
        scratch_shapes=scratch,
        compiler_params=pltpu.CompilerParams(
            collective_id=0, has_side_effects=True, vmem_limit_bytes=32 * 1024 * 1024
        ),
    )(velocity, column_state, height_index, rotor_mask, thrust, table)


def solution(mesh):
    in_specs = (
        P(None, "gz", "gx", "gy"),
        P(None, None, "gx", ("gy", "gz")),
        P("gx", "gy"),
        P("gz", "gx", "gy"),
        P(),
    )
    out_specs = (P(None, "gz", "gx", "gy"), P(None, None, "gx", ("gy", "gz")))
    run = functools.partial(local, mesh.shape["gx"], mesh.shape["gy"], mesh.shape["gz"])
    return jax.shard_map(run, mesh=mesh, in_specs=in_specs, out_specs=out_specs, check_vma=False)
```

```python
import functools
import math

import jax
import jax.numpy as jnp
import numpy as np
from jax import lax
from jax.experimental import pallas as pl
from jax.experimental.pallas import tpu as pltpu
from jax.sharding import PartitionSpec as P

LEVELS = 8
LANES = 128
MESH = pl.DeviceIdType.MESH
CHUNKS = 4

time_step = 0.1
viscosity = 0.02
smag_coeff = 0.0289
karman = 0.41
wall_step = 0.05
stretch = 3.0


def column_constants(points):
    ladder = np.arange(points, dtype=np.float64) / (points - 1)
    spacing = (np.exp(stretch * ladder) - 1.0) / (math.exp(stretch) - 1.0)
    gap = spacing[1:] - spacing[:-1]
    middle = 0.5 * (spacing[1:] + spacing[:-1])
    laminar = viscosity / gap
    eddy = (karman * middle / gap) ** 2
    volume = np.zeros_like(gap)
    volume[1:] = 0.5 * (gap[1:] + gap[:-1]) / wall_step
    return [[float(np.float32(v)) for v in row] for row in (laminar, eddy, volume)]


def kernel(
    sizes,
    v_hbm, s_hbm, h_hbm, m_hbm, t_hbm,
    adv_ref, fresh_ref,
    v, s, h, mask, thrust_ref, tab_ref, eddy, coef_e, coef_f,
    xlo, xhi, zhalo, ypack_lo, ypack_hi, ylo, yhi,
    stage, tops, back, walls, plane,
    load_sem, x_send, x_recv, y_send, y_recv, z_send, z_recv, t_send, t_recv, w_send, w_recv,
):
    n_gx, n_gy, n_gz, layers, rows, width, points, cols = sizes
    group = n_gy * n_gz
    block = width // group
    tiles = width // LANES
    gx, gy, gz = lax.axis_index("gx"), lax.axis_index("gy"), lax.axis_index("gz")
    me = gy * n_gz + gz
    left, right = lax.rem(gx + n_gx - 1, n_gx), lax.rem(gx + 1, n_gx)
    below, above = lax.rem(gy + n_gy - 1, n_gy), lax.rem(gy + 1, n_gy)
    at_wall = gz == 0

    loads = [
        pltpu.make_async_copy(h_hbm, h, load_sem.at[0]),
        pltpu.make_async_copy(
            v_hbm.at[pl.ds(0, 2), pl.ds(0, LEVELS + 1)], v.at[pl.ds(0, 2), pl.ds(0, LEVELS + 1)], load_sem.at[1]
        ),
        pltpu.make_async_copy(
            v_hbm.at[pl.ds(0, 2), pl.ds(LEVELS + 1, layers - LEVELS - 1)],
            v.at[pl.ds(0, 2), pl.ds(LEVELS + 1, layers - LEVELS - 1)],
            load_sem.at[2],
        ),
        pltpu.make_async_copy(v_hbm.at[2], v.at[2], load_sem.at[3]),
        pltpu.make_async_copy(s_hbm, s, load_sem.at[4]),
        pltpu.make_async_copy(m_hbm.at[pl.ds(2, 8)], mask, load_sem.at[5]),
        pltpu.make_async_copy(t_hbm, thrust_ref, load_sem.at[6]),
    ]
    for load in loads:
        load.start()

    barrier = pltpu.get_barrier_semaphore()
    for side in (left, right):
        pl.semaphore_signal(barrier, inc=1, device_id=(side, gy, gz), device_id_type=MESH)
    for d in range(1, group):
        r = lax.rem(me + d, group)
        pl.semaphore_signal(barrier, inc=1, device_id=(gx, r // n_gz, r % n_gz), device_id_type=MESH)

    for j, entries in enumerate(column_constants(points)):
        for i, entry in enumerate(entries):
            tab_ref[j, i] = entry

    loads[0].wait()
    loads[1].wait()

    @pl.when(at_wall)
    def _():
        height = h[...]
        for c in range(2):
            picked = v[c, LEVELS]
            for level in range(1, LEVELS):
                picked = jnp.where(height == level, v[c, level], picked)
            for r in range(group):
                j, off = (r * block) // LANES, (r * block) % LANES
                part = picked[:, j * LANES : (j + 1) * LANES]
                if off:
                    part = pltpu.roll(part, LANES - off, 1)
                stage[r, c] = part
        sample_height = height.astype(jnp.float32) + 0.5
        for r in range(group):
            j, off = (r * block) // LANES, (r * block) % LANES
            part = sample_height[:, j * LANES : (j + 1) * LANES]
            if off:
                part = pltpu.roll(part, LANES - off, 1)
            stage[r, 2] = part
        tops[gy] = stage[me]

    pl.semaphore_wait(barrier, 2 + group - 1)

    def top_send(d):
        r = lax.rem(me + d, group)
        return pltpu.make_async_remote_copy(
            src_ref=stage.at[r], dst_ref=tops.at[gy], send_sem=t_send.at[d], recv_sem=t_recv.at[gy],
            device_id=(gx, r // n_gz, r % n_gz), device_id_type=MESH,
        )

    @pl.when(at_wall)
    def _():
        for d in range(1, group):
            top_send(d).start()

    def x_copies(k):
        depth = layers // CHUNKS
        zs = pl.ds((CHUNKS - 1 - k) * depth, depth)
        to_right = pltpu.make_async_remote_copy(
            src_ref=v_hbm.at[:, zs, pl.ds(rows - 1, 1)], dst_ref=xlo.at[:, zs],
            send_sem=x_send.at[2 * k], recv_sem=x_recv.at[2 * k],
            device_id=(right, gy, gz), device_id_type=MESH,
        )
        to_left = pltpu.make_async_remote_copy(
            src_ref=v_hbm.at[:, zs, pl.ds(0, 1)], dst_ref=xhi.at[:, zs],
            send_sem=x_send.at[2 * k + 1], recv_sem=x_recv.at[2 * k + 1],
            device_id=(left, gy, gz), device_id_type=MESH,
        )
        return to_right, to_left

    for k in range(CHUNKS):
        for copy in x_copies(k):
            copy.start()

    edge = (layers - 1) * (1 - gz)
    z_copy = pltpu.make_async_remote_copy(
        src_ref=v_hbm.at[:, edge], dst_ref=zhalo, send_sem=z_send.at[0], recv_sem=z_recv.at[0],
        device_id=(gx, gy, 1 - gz), device_id_type=MESH,
    )
    z_copy.start()

    loads[2].wait()
    loads[3].wait()
    lane = lax.broadcasted_iota(jnp.int32, (rows, LANES), 1)

    def pack(k, carry):
        low, high = carry
        c, z = k // layers, k % layers
        low = jnp.where(lane == k, pltpu.roll(v[c, z, :, :LANES], k, 1), low)
        high = jnp.where(lane == k, pltpu.roll(v[c, z, :, width - LANES :], k + 1, 1), high)
        return low, high

    zeros = jnp.zeros((rows, LANES), jnp.float32)
    low, high = lax.fori_loop(0, 3 * layers, pack, (zeros, zeros), unroll=4)
    ypack_lo[...] = low
    ypack_hi[...] = high
    y_copies = [
        pltpu.make_async_remote_copy(
            src_ref=ypack_hi, dst_ref=ylo, send_sem=y_send.at[0], recv_sem=y_recv.at[0],
            device_id=(gx, above, gz), device_id_type=MESH,
        ),
        pltpu.make_async_remote_copy(
            src_ref=ypack_lo, dst_ref=yhi, send_sem=y_send.at[1], recv_sem=y_recv.at[1],
            device_id=(gx, below, gz), device_id_type=MESH,
        ),
    ]
    for copy in y_copies:
        copy.start()

    loads[4].wait()

    def shear(i, carry):
        du = s[0, i + 1] - s[0, i]
        dv = s[1, i + 1] - s[1, i]
        eddy[i] = tab_ref[1, i] * jnp.sqrt(du * du + dv * dv + 1e-06)
        return carry

    lax.fori_loop(0, points - 1, shear, 0, unroll=3)

    def top_wait(src):
        pltpu.make_async_remote_copy(
            src_ref=stage.at[0], dst_ref=tops.at[src], send_sem=t_send.at[0], recv_sem=t_recv.at[src],
            device_id=(gx, gy, 1 - gz), device_id_type=MESH,
        ).wait_recv()

    for src in range(n_gy):

        @pl.when(me != src * n_gz)
        def _():
            top_wait(src)

    lane_wide = lax.broadcasted_iota(jnp.int32, (rows, cols), 1)
    halves = cols // LANES

    def interleave(field):
        parts = []
        for half in range(halves):
            source = (lane + half * LANES) // n_gy
            owner = (lane + half * LANES) % n_gy
            out = None
            for src in range(n_gy):
                got = jnp.take_along_axis(tops[src, field], source, axis=1, mode="promise_in_bounds")
                out = got if out is None else jnp.where(owner == src, got, out)
            parts.append(out)
        return jnp.concatenate(parts, axis=1)

    top_u, top_v, height = interleave(0), interleave(1), interleave(2)
    inv_height = 1.0 / height

    last = points - 1
    fresh_ref[0, last] = top_u
    fresh_ref[1, last] = top_v
    fresh_ref[0, 0] = jnp.zeros_like(top_u)
    fresh_ref[1, 0] = jnp.zeros_like(top_u)

    def eliminate(k, carry):
        share, cond, f_u, f_v = carry
        i = last - 1 - k
        cond_low = tab_ref[0, i - 1] * inv_height + eddy[i - 1]
        volume = tab_ref[2, i] * height
        held = volume + share
        inverse = 1.0 / (held + cond_low)
        f_u = (volume * s[0, i] + cond * f_u) * inverse
        f_v = (volume * s[1, i] + cond * f_v) * inverse
        coef_e[i] = cond_low * inverse
        coef_f[0, i] = f_u
        coef_f[1, i] = f_v
        return cond_low * (held * inverse), cond_low, f_u, f_v

    cond_top = tab_ref[0, last - 1] * inv_height + eddy[last - 1]
    _, cond, f_u, f_v = lax.fori_loop(0, points - 2, eliminate, (cond_top, cond_top, top_u, top_v), unroll=2)
    stress = (cond * f_u, cond * f_v)

    for src in range(n_gy):
        index = lane * n_gy + src
        index = jnp.where(index < cols, index, 0)
        for c in range(2):
            out = None
            for half in range(halves):
                got = jnp.take_along_axis(
                    stress[c][:, half * LANES : (half + 1) * LANES], index % LANES, axis=1, mode="promise_in_bounds"
                )
                out = got if out is None else jnp.where(index // LANES == half, got, out)
            back[src, c] = out

    def wall_send(src):
        return pltpu.make_async_remote_copy(
            src_ref=back.at[src], dst_ref=walls.at[me], send_sem=w_send.at[src], recv_sem=w_recv.at[me],
            device_id=(gx, src, 0), device_id_type=MESH,
        )

    for src in range(n_gy):

        @pl.when(me != src * n_gz)
        def _():
            wall_send(src).start()

    @pl.when(at_wall)
    def _():
        walls[me] = back[gy]

    def substitute(k, carry):
        u, w = carry
        i = k + 1
        e = coef_e[i]
        u = e * u + coef_f[0, i]
        w = e * w + coef_f[1, i]
        fresh_ref[0, i] = u
        fresh_ref[1, i] = w
        return u, w

    zero = jnp.zeros_like(top_u)
    lax.fori_loop(0, points - 2, substitute, (zero, zero), unroll=2)

    for copy in y_copies:
        copy.wait_recv()
    z_copy.wait_recv()
    loads[5].wait()
    loads[6].wait()

    disks = mask[0]
    for k in range(1, 8):
        disks = jnp.maximum(disks, mask[k])
    force = jnp.zeros((rows, width), jnp.float32)
    for k in range(8):
        force = force + jnp.where(disks == k + 1, thrust_ref[k], 0.0)
    plane[...] = force * time_step

    row = lax.broadcasted_iota(jnp.int32, (rows, width), 0)
    col = lax.broadcasted_iota(jnp.int32, (rows, width), 1)

    def layer(z, below_v, above_v, wall):
        vel, xn, xp, yn, yp = [], [], [], [], []
        for c in range(3):
            here = v[c, z]
            vel.append(here)
            xp.append(jnp.where(row == 0, xlo[c, z], pltpu.roll(here, 1, 0)))
            xn.append(jnp.where(row == rows - 1, xhi[c, z], pltpu.roll(here, rows - 1, 0)))
            slot = c * layers + z
            low = pltpu.roll(ylo[...], LANES - slot, 1)
            high = pltpu.roll(yhi[...], LANES - 1 - slot, 1)
            low = jnp.concatenate([low] * tiles, axis=1)
            high = jnp.concatenate([high] * tiles, axis=1)
            yp.append(jnp.where(col == 0, low, pltpu.roll(here, 1, 1)))
            yn.append(jnp.where(col == width - 1, high, pltpu.roll(here, width - 1, 1)))
        zn, zp = above_v, below_v
        d_x = [xn[c] - xp[c] for c in range(3)]
        d_y = [yn[c] - yp[c] for c in range(3)]
        d_z = [zn[c] - zp[c] for c in range(3)]
        diag = d_x[0] * d_x[0] + d_y[1] * d_y[1] + d_z[2] * d_z[2]
        s_xy, s_xz, s_yz = d_y[0] + d_x[1], d_z[0] + d_x[2], d_z[1] + d_y[2]
        cross = s_xy * s_xy + s_xz * s_xz + s_yz * s_yz
        strain = jnp.sqrt(0.5 * diag + (0.25 * cross + 1e-06))
        viscous = time_step * viscosity + (time_step * smag_coeff) * strain
        for c in range(3):
            total = (xn[c] + xp[c]) + (yn[c] + yp[c]) + (zn[c] + zp[c])
            flux = (
                (xn[c] * xn[0] - xp[c] * xp[0]) + (yn[c] * yn[1] - yp[c] * yp[1]) + (zn[c] * zn[2] - zp[c] * zp[2])
            )
            lap = total - 6.0 * vel[c]
            if wall is not None and c < 2:
                lap = lap + wall[0] * vel[c]
            out = vel[c] + (viscous * lap - (0.5 * time_step) * flux)
            if wall is not None and c < 2:
                out = out - time_step * wall[1][c]
            adv_ref[c, z] = out

    def velocity_at(z):
        return [v[c, z] for c in range(3)]

    def x_wait(k):
        for copy in x_copies(k):
            copy.wait_recv()

    depth = layers // CHUNKS
    x_wait(0)
    bottom = at_wall.astype(jnp.float32)
    layer(layers - 1, velocity_at(layers - 2), [zhalo[c] * bottom for c in range(3)], None)

    def inner(z, carry):
        layer(z, velocity_at(z - 1), velocity_at(z + 1), None)
        return carry

    lax.fori_loop(layers - depth, layers - 1, inner, 0)
    for k in range(1, CHUNKS):
        x_wait(k)
        low = (CHUNKS - 1 - k) * depth
        lax.fori_loop(max(low, 1), low + depth, inner, 0)

    def wall_wait(r):
        pltpu.make_async_remote_copy(
            src_ref=back.at[0], dst_ref=walls.at[r], send_sem=w_send.at[0], recv_sem=w_recv.at[r],
            device_id=(gx, gy, 1 - gz), device_id_type=MESH,
        ).wait_recv()

    @pl.when(at_wall)
    def _():
        for r in range(group):

            @pl.when(me != r)
            def _():
                wall_wait(r)

        wall = []
        for c in range(2):
            parts = []
            for j in range(tiles):
                out = None
                for r in range(group):
                    if (r * block) // LANES == j:
                        off = (r * block) % LANES
                        got = walls[r, c]
                        if off:
                            got = pltpu.roll(got, off, 1)
                        out = got if out is None else jnp.where(lane >= off, got, out)
                parts.append(out)
            wall.append(jnp.concatenate(parts, axis=1))
        layer(0, [jnp.zeros((rows, width), jnp.float32)] * 3, velocity_at(1), (1.0, wall))

        for k in range(8):
            adv_ref[2, 2 + k] = adv_ref[2, 2 + k] - jnp.where(mask[k] != 0, plane[...], 0.0)

    @pl.when(jnp.logical_not(at_wall))
    def _():
        layer(0, [zhalo[c] for c in range(3)], velocity_at(1), None)

    @pl.when(at_wall)
    def _():
        for d in range(1, group):
            top_send(d).wait_send()

    for src in range(n_gy):

        @pl.when(me != src * n_gz)
        def _():
            wall_send(src).wait_send()

    for k in range(CHUNKS):
        for copy in x_copies(k):
            copy.wait_send()
    for copy in y_copies:
        copy.wait_send()
    z_copy.wait_send()


def local(n_gx, n_gy, n_gz, velocity, column_state, height_index, rotor_mask, thrust):
    _, layers, rows, width = velocity.shape
    _, points, _, cols = column_state.shape
    group = n_gy * n_gz
    hbm_spec = pl.BlockSpec(memory_space=pltpu.HBM)
    vmem_spec = pl.BlockSpec(memory_space=pltpu.VMEM)
    f32 = jnp.float32
    dma = pltpu.SemaphoreType.DMA
    scratch = [
        pltpu.VMEM(velocity.shape, f32),
        pltpu.VMEM(column_state.shape, f32),
        pltpu.VMEM(height_index.shape, jnp.int32),
        pltpu.VMEM((8, rows, width), jnp.int32),
        pltpu.SMEM(thrust.shape, f32),
        pltpu.SMEM((3, points - 1), f32),
        pltpu.VMEM((points - 1, rows, cols), f32),
        pltpu.VMEM((points - 1, rows, cols), f32),
        pltpu.VMEM((2, points - 1, rows, cols), f32),
        pltpu.VMEM((3, layers, 1, width), f32),
        pltpu.VMEM((3, layers, 1, width), f32),
        pltpu.VMEM((3, rows, width), f32),
        pltpu.VMEM((rows, LANES), f32),
        pltpu.VMEM((rows, LANES), f32),
        pltpu.VMEM((rows, LANES), f32),
        pltpu.VMEM((rows, LANES), f32),
        pltpu.VMEM((group, 3, rows, LANES), f32),
        pltpu.VMEM((n_gy, 3, rows, LANES), f32),
        pltpu.VMEM((n_gy, 2, rows, LANES), f32),
        pltpu.VMEM((group, 2, rows, LANES), f32),
        pltpu.VMEM((rows, width), f32),
        dma((7,)),
        dma((2 * CHUNKS,)), dma((2 * CHUNKS,)),
        dma((2,)), dma((2,)),
        dma((1,)), dma((1,)),
        dma((group,)), dma((n_gy,)),
        dma((n_gy,)), dma((group,)),
    ]
    sizes = (n_gx, n_gy, n_gz, layers, rows, width, points, cols)
    return pl.pallas_call(
        functools.partial(kernel, sizes),
        out_shape=(
            jax.ShapeDtypeStruct(velocity.shape, f32),
            jax.ShapeDtypeStruct(column_state.shape, f32),
        ),
        in_specs=[hbm_spec] * 5,
        out_specs=(vmem_spec, vmem_spec),
        scratch_shapes=scratch,
        compiler_params=pltpu.CompilerParams(
            collective_id=0, has_side_effects=True, vmem_limit_bytes=32 * 1024 * 1024
        ),
    )(*[pltpu.with_memory_space_constraint(a, pltpu.HBM) for a in (velocity, column_state, height_index, rotor_mask, thrust)])


def solution(mesh):
    in_specs = (
        P(None, "gz", "gx", "gy"),
        P(None, None, "gx", ("gy", "gz")),
        P("gx", "gy"),
        P("gz", "gx", "gy"),
        P(),
    )
    out_specs = (P(None, "gz", "gx", "gy"), P(None, None, "gx", ("gy", "gz")))
    run = functools.partial(local, mesh.shape["gx"], mesh.shape["gy"], mesh.shape["gz"])
    return jax.shard_map(run, mesh=mesh, in_specs=in_specs, out_specs=out_specs, check_vma=False)
```

```python
import functools
import math

import jax
import jax.numpy as jnp
import numpy as np
from jax import lax
from jax.experimental import pallas as pl
from jax.experimental.pallas import tpu as pltpu
from jax.sharding import PartitionSpec as P

LEVELS = 8
LANES = 128
MESH = pl.DeviceIdType.MESH
CHUNKS = 4

time_step = 0.1
viscosity = 0.02
smag_coeff = 0.0289
karman = 0.41
wall_step = 0.05
stretch = 3.0


def column_constants(points):
    ladder = np.arange(points, dtype=np.float64) / (points - 1)
    spacing = (np.exp(stretch * ladder) - 1.0) / (math.exp(stretch) - 1.0)
    gap = spacing[1:] - spacing[:-1]
    middle = 0.5 * (spacing[1:] + spacing[:-1])
    laminar = viscosity / gap
    eddy = (karman * middle / gap) ** 2
    volume = np.zeros_like(gap)
    volume[1:] = 0.5 * (gap[1:] + gap[:-1]) / wall_step
    return [[float(np.float32(v)) for v in row] for row in (laminar, eddy, volume)]


def kernel(
    sizes,
    v_hbm, s_hbm, h_hbm, m_hbm, t_hbm,
    adv_ref, fresh_ref,
    v, s, h, mask, thrust_ref, tab_ref, eddy, coef_e, coef_f,
    xlo, xhi, zhalo, ypack_lo, ypack_hi, ylo, yhi,
    stage, tops, back, walls, plane,
    load_sem, x_send, x_recv, y_send, y_recv, z_send, z_recv, t_send, t_recv, w_send, w_recv, ready,
):
    n_gx, n_gy, n_gz, layers, rows, width, points, cols = sizes
    group = n_gy * n_gz
    block = width // group
    tiles = width // LANES
    gx, gy, gz = lax.axis_index("gx"), lax.axis_index("gy"), lax.axis_index("gz")
    me = gy * n_gz + gz
    left, right = lax.rem(gx + n_gx - 1, n_gx), lax.rem(gx + 1, n_gx)
    below, above = lax.rem(gy + n_gy - 1, n_gy), lax.rem(gy + 1, n_gy)
    at_wall = gz == 0

    loads = [
        pltpu.make_async_copy(h_hbm, h, load_sem.at[0]),
        pltpu.make_async_copy(
            v_hbm.at[pl.ds(0, 2), pl.ds(0, LEVELS + 1)], v.at[pl.ds(0, 2), pl.ds(0, LEVELS + 1)], load_sem.at[1]
        ),
        pltpu.make_async_copy(
            v_hbm.at[pl.ds(0, 2), pl.ds(LEVELS + 1, layers - LEVELS - 1)],
            v.at[pl.ds(0, 2), pl.ds(LEVELS + 1, layers - LEVELS - 1)],
            load_sem.at[2],
        ),
        pltpu.make_async_copy(v_hbm.at[2], v.at[2], load_sem.at[3]),
        pltpu.make_async_copy(s_hbm, s, load_sem.at[4]),
        pltpu.make_async_copy(m_hbm.at[pl.ds(2, 8)], mask, load_sem.at[5]),
        pltpu.make_async_copy(t_hbm, thrust_ref, load_sem.at[6]),
    ]
    for load in loads:
        load.start()

    barrier = pltpu.get_barrier_semaphore()
    for side in (left, right):

        @pl.when(side != 0)
        def _():
            pl.semaphore_signal(barrier, inc=1, device_id=(side, gy, gz), device_id_type=MESH)

    for d in range(1, group):
        r = lax.rem(me + d, group)
        pl.semaphore_signal(barrier, inc=1, device_id=(gx, r // n_gz, r % n_gz), device_id_type=MESH)

    for j, entries in enumerate(column_constants(points)):
        for i, entry in enumerate(entries):
            tab_ref[j, i] = entry

    loads[0].wait()
    loads[1].wait()

    @pl.when(at_wall)
    def _():
        height = h[...]
        for c in range(2):
            picked = v[c, LEVELS]
            for level in range(1, LEVELS):
                picked = jnp.where(height == level, v[c, level], picked)
            for r in range(group):
                j, off = (r * block) // LANES, (r * block) % LANES
                part = picked[:, j * LANES : (j + 1) * LANES]
                if off:
                    part = pltpu.roll(part, LANES - off, 1)
                stage[r, c] = part
        sample_height = height.astype(jnp.float32) + 0.5
        for r in range(group):
            j, off = (r * block) // LANES, (r * block) % LANES
            part = sample_height[:, j * LANES : (j + 1) * LANES]
            if off:
                part = pltpu.roll(part, LANES - off, 1)
            stage[r, 2] = part
        tops[gy] = stage[me]

    first = gx == 0

    @pl.when(first)
    def _():
        pl.semaphore_wait(barrier, group - 1)

    @pl.when(jnp.logical_not(first))
    def _():
        pl.semaphore_wait(barrier, 2 + group - 1)
        for side in (left, right):

            @pl.when(side == 0)
            def _():
                pl.semaphore_signal(ready, inc=1, device_id=(side, gy, gz), device_id_type=MESH)


    def top_send(d):
        r = lax.rem(me + d, group)
        return pltpu.make_async_remote_copy(
            src_ref=stage.at[r], dst_ref=tops.at[gy], send_sem=t_send.at[d], recv_sem=t_recv.at[gy],
            device_id=(gx, r // n_gz, r % n_gz), device_id_type=MESH,
        )

    @pl.when(at_wall)
    def _():
        for d in range(1, group):
            top_send(d).start()

    def x_copies(k):
        depth = layers // CHUNKS
        zs = pl.ds((CHUNKS - 1 - k) * depth, depth)
        to_right = pltpu.make_async_remote_copy(
            src_ref=v_hbm.at[:, zs, pl.ds(rows - 1, 1)], dst_ref=xlo.at[:, zs],
            send_sem=x_send.at[2 * k], recv_sem=x_recv.at[2 * k],
            device_id=(right, gy, gz), device_id_type=MESH,
        )
        to_left = pltpu.make_async_remote_copy(
            src_ref=v_hbm.at[:, zs, pl.ds(0, 1)], dst_ref=xhi.at[:, zs],
            send_sem=x_send.at[2 * k + 1], recv_sem=x_recv.at[2 * k + 1],
            device_id=(left, gy, gz), device_id_type=MESH,
        )
        return to_right, to_left

    @pl.when(jnp.logical_not(first))
    def _():
        for k in range(CHUNKS):
            for copy in x_copies(k):
                copy.start()

    edge = (layers - 1) * (1 - gz)
    z_copy = pltpu.make_async_remote_copy(
        src_ref=v_hbm.at[:, edge], dst_ref=zhalo, send_sem=z_send.at[0], recv_sem=z_recv.at[0],
        device_id=(gx, gy, 1 - gz), device_id_type=MESH,
    )
    z_copy.start()

    loads[2].wait()
    loads[3].wait()
    lane = lax.broadcasted_iota(jnp.int32, (rows, LANES), 1)

    def pack(k, carry):
        low, high = carry
        c, z = k // layers, k % layers
        low = jnp.where(lane == k, pltpu.roll(v[c, z, :, :LANES], k, 1), low)
        high = jnp.where(lane == k, pltpu.roll(v[c, z, :, width - LANES :], k + 1, 1), high)
        return low, high

    zeros = jnp.zeros((rows, LANES), jnp.float32)
    low, high = lax.fori_loop(0, 3 * layers, pack, (zeros, zeros), unroll=4)
    ypack_lo[...] = low
    ypack_hi[...] = high
    y_copies = [
        pltpu.make_async_remote_copy(
            src_ref=ypack_hi, dst_ref=ylo, send_sem=y_send.at[0], recv_sem=y_recv.at[0],
            device_id=(gx, above, gz), device_id_type=MESH,
        ),
        pltpu.make_async_remote_copy(
            src_ref=ypack_lo, dst_ref=yhi, send_sem=y_send.at[1], recv_sem=y_recv.at[1],
            device_id=(gx, below, gz), device_id_type=MESH,
        ),
    ]
    for copy in y_copies:
        copy.start()

    loads[4].wait()

    def shear(i, carry):
        du = s[0, i + 1] - s[0, i]
        dv = s[1, i + 1] - s[1, i]
        eddy[i] = tab_ref[1, i] * jnp.sqrt(du * du + dv * dv + 1e-06)
        return carry

    lax.fori_loop(0, points - 1, shear, 0, unroll=3)

    def top_wait(src):
        pltpu.make_async_remote_copy(
            src_ref=stage.at[0], dst_ref=tops.at[src], send_sem=t_send.at[0], recv_sem=t_recv.at[src],
            device_id=(gx, gy, 1 - gz), device_id_type=MESH,
        ).wait_recv()

    for src in range(n_gy):

        @pl.when(me != src * n_gz)
        def _():
            top_wait(src)

    lane_wide = lax.broadcasted_iota(jnp.int32, (rows, cols), 1)
    halves = cols // LANES

    def interleave(field):
        parts = []
        for half in range(halves):
            source = (lane + half * LANES) // n_gy
            owner = (lane + half * LANES) % n_gy
            out = None
            for src in range(n_gy):
                got = jnp.take_along_axis(tops[src, field], source, axis=1, mode="promise_in_bounds")
                out = got if out is None else jnp.where(owner == src, got, out)
            parts.append(out)
        return jnp.concatenate(parts, axis=1)

    top_u, top_v, height = interleave(0), interleave(1), interleave(2)
    inv_height = 1.0 / height

    last = points - 1
    fresh_ref[0, last] = top_u
    fresh_ref[1, last] = top_v
    fresh_ref[0, 0] = jnp.zeros_like(top_u)
    fresh_ref[1, 0] = jnp.zeros_like(top_u)

    def eliminate(k, carry):
        share, cond, f_u, f_v = carry
        i = last - 1 - k
        cond_low = tab_ref[0, i - 1] * inv_height + eddy[i - 1]
        volume = tab_ref[2, i] * height
        held = volume + share
        inverse = 1.0 / (held + cond_low)
        f_u = (volume * s[0, i] + cond * f_u) * inverse
        f_v = (volume * s[1, i] + cond * f_v) * inverse
        coef_e[i] = cond_low * inverse
        coef_f[0, i] = f_u
        coef_f[1, i] = f_v
        return cond_low * (held * inverse), cond_low, f_u, f_v

    cond_top = tab_ref[0, last - 1] * inv_height + eddy[last - 1]
    _, cond, f_u, f_v = lax.fori_loop(0, points - 2, eliminate, (cond_top, cond_top, top_u, top_v), unroll=2)
    stress = (cond * f_u, cond * f_v)

    for src in range(n_gy):
        index = lane * n_gy + src
        index = jnp.where(index < cols, index, 0)
        for c in range(2):
            out = None
            for half in range(halves):
                got = jnp.take_along_axis(
                    stress[c][:, half * LANES : (half + 1) * LANES], index % LANES, axis=1, mode="promise_in_bounds"
                )
                out = got if out is None else jnp.where(index // LANES == half, got, out)
            back[src, c] = out

    def wall_send(src):
        return pltpu.make_async_remote_copy(
            src_ref=back.at[src], dst_ref=walls.at[me], send_sem=w_send.at[src], recv_sem=w_recv.at[me],
            device_id=(gx, src, 0), device_id_type=MESH,
        )

    for src in range(n_gy):

        @pl.when(me != src * n_gz)
        def _():
            wall_send(src).start()

    @pl.when(at_wall)
    def _():
        walls[me] = back[gy]

    @pl.when(first)
    def _():
        pl.semaphore_wait(ready, 2)
        for k in range(CHUNKS):
            for copy in x_copies(k):
                copy.start()

    def substitute(k, carry):
        u, w = carry
        i = k + 1
        e = coef_e[i]
        u = e * u + coef_f[0, i]
        w = e * w + coef_f[1, i]
        fresh_ref[0, i] = u
        fresh_ref[1, i] = w
        return u, w

    zero = jnp.zeros_like(top_u)
    lax.fori_loop(0, points - 2, substitute, (zero, zero), unroll=2)

    for copy in y_copies:
        copy.wait_recv()
    z_copy.wait_recv()
    loads[5].wait()
    loads[6].wait()

    disks = mask[0]
    for k in range(1, 8):
        disks = jnp.maximum(disks, mask[k])
    force = jnp.zeros((rows, width), jnp.float32)
    for k in range(8):
        force = force + jnp.where(disks == k + 1, thrust_ref[k], 0.0)
    plane[...] = force * time_step

    row = lax.broadcasted_iota(jnp.int32, (rows, width), 0)
    col = lax.broadcasted_iota(jnp.int32, (rows, width), 1)

    def layer(z, below_v, above_v, wall):
        vel, xn, xp, yn, yp = [], [], [], [], []
        for c in range(3):
            here = v[c, z]
            vel.append(here)
            xp.append(jnp.where(row == 0, xlo[c, z], pltpu.roll(here, 1, 0)))
            xn.append(jnp.where(row == rows - 1, xhi[c, z], pltpu.roll(here, rows - 1, 0)))
            slot = c * layers + z
            low = pltpu.roll(ylo[...], LANES - slot, 1)
            high = pltpu.roll(yhi[...], LANES - 1 - slot, 1)
            low = jnp.concatenate([low] * tiles, axis=1)
            high = jnp.concatenate([high] * tiles, axis=1)
            yp.append(jnp.where(col == 0, low, pltpu.roll(here, 1, 1)))
            yn.append(jnp.where(col == width - 1, high, pltpu.roll(here, width - 1, 1)))
        zn, zp = above_v, below_v
        d_x = [xn[c] - xp[c] for c in range(3)]
        d_y = [yn[c] - yp[c] for c in range(3)]
        d_z = [zn[c] - zp[c] for c in range(3)]
        diag = d_x[0] * d_x[0] + d_y[1] * d_y[1] + d_z[2] * d_z[2]
        s_xy, s_xz, s_yz = d_y[0] + d_x[1], d_z[0] + d_x[2], d_z[1] + d_y[2]
        cross = s_xy * s_xy + s_xz * s_xz + s_yz * s_yz
        strain = jnp.sqrt(0.5 * diag + (0.25 * cross + 1e-06))
        viscous = time_step * viscosity + (time_step * smag_coeff) * strain
        for c in range(3):
            total = (xn[c] + xp[c]) + (yn[c] + yp[c]) + (zn[c] + zp[c])
            flux = (
                (xn[c] * xn[0] - xp[c] * xp[0]) + (yn[c] * yn[1] - yp[c] * yp[1]) + (zn[c] * zn[2] - zp[c] * zp[2])
            )
            lap = total - 6.0 * vel[c]
            if wall is not None and c < 2:
                lap = lap + wall[0] * vel[c]
            out = vel[c] + (viscous * lap - (0.5 * time_step) * flux)
            if wall is not None and c < 2:
                out = out - time_step * wall[1][c]
            adv_ref[c, z] = out

    def velocity_at(z):
        return [v[c, z] for c in range(3)]

    def x_wait(k):
        for copy in x_copies(k):
            copy.wait_recv()

    depth = layers // CHUNKS
    x_wait(0)
    bottom = at_wall.astype(jnp.float32)
    layer(layers - 1, velocity_at(layers - 2), [zhalo[c] * bottom for c in range(3)], None)

    def inner(z, carry):
        layer(z, velocity_at(z - 1), velocity_at(z + 1), None)
        return carry

    lax.fori_loop(max(layers - depth, 1), layers - 1, inner, 0)
    for k in range(1, CHUNKS):
        x_wait(k)
        low = (CHUNKS - 1 - k) * depth
        lax.fori_loop(max(low, 1), low + depth, inner, 0)

    def wall_wait(r):
        pltpu.make_async_remote_copy(
            src_ref=back.at[0], dst_ref=walls.at[r], send_sem=w_send.at[0], recv_sem=w_recv.at[r],
            device_id=(gx, gy, 1 - gz), device_id_type=MESH,
        ).wait_recv()

    @pl.when(at_wall)
    def _():
        for r in range(group):

            @pl.when(me != r)
            def _():
                wall_wait(r)

        wall = []
        for c in range(2):
            parts = []
            for j in range(tiles):
                out = None
                for r in range(group):
                    if (r * block) // LANES == j:
                        off = (r * block) % LANES
                        got = walls[r, c]
                        if off:
                            got = pltpu.roll(got, off, 1)
                        out = got if out is None else jnp.where(lane >= off, got, out)
                parts.append(out)
            wall.append(jnp.concatenate(parts, axis=1))
        layer(0, [jnp.zeros((rows, width), jnp.float32)] * 3, velocity_at(1), (1.0, wall))

        for k in range(8):
            adv_ref[2, 2 + k] = adv_ref[2, 2 + k] - jnp.where(mask[k] != 0, plane[...], 0.0)

    @pl.when(jnp.logical_not(at_wall))
    def _():
        layer(0, [zhalo[c] for c in range(3)], velocity_at(1), None)

    @pl.when(at_wall)
    def _():
        for d in range(1, group):
            top_send(d).wait_send()

    for src in range(n_gy):

        @pl.when(me != src * n_gz)
        def _():
            wall_send(src).wait_send()

    for k in range(CHUNKS):
        for copy in x_copies(k):
            copy.wait_send()
    for copy in y_copies:
        copy.wait_send()
    z_copy.wait_send()


def write_out(advanced, fresh, advanced_hbm, fresh_hbm, sem):
    copies = [pltpu.make_async_copy(fresh.at[c], fresh_hbm.at[c], sem.at[c]) for c in range(2)]
    copies += [pltpu.make_async_copy(advanced.at[c], advanced_hbm.at[c], sem.at[2 + c]) for c in range(3)]
    for copy in copies:
        copy.start()
    for copy in copies:
        copy.wait()


def local(n_gx, n_gy, n_gz, velocity, column_state, height_index, rotor_mask, thrust):
    _, layers, rows, width = velocity.shape
    _, points, _, cols = column_state.shape
    group = n_gy * n_gz
    hbm_spec = pl.BlockSpec(memory_space=pltpu.HBM)
    vmem_spec = pl.BlockSpec(memory_space=pltpu.VMEM)
    f32 = jnp.float32
    dma = pltpu.SemaphoreType.DMA
    scratch = [
        pltpu.VMEM(velocity.shape, f32),
        pltpu.VMEM(column_state.shape, f32),
        pltpu.VMEM(height_index.shape, jnp.int32),
        pltpu.VMEM((8, rows, width), jnp.int32),
        pltpu.SMEM(thrust.shape, f32),
        pltpu.SMEM((3, points - 1), f32),
        pltpu.VMEM((points - 1, rows, cols), f32),
        pltpu.VMEM((points - 1, rows, cols), f32),
        pltpu.VMEM((2, points - 1, rows, cols), f32),
        pltpu.VMEM((3, layers, 1, width), f32),
        pltpu.VMEM((3, layers, 1, width), f32),
        pltpu.VMEM((3, rows, width), f32),
        pltpu.VMEM((rows, LANES), f32),
        pltpu.VMEM((rows, LANES), f32),
        pltpu.VMEM((rows, LANES), f32),
        pltpu.VMEM((rows, LANES), f32),
        pltpu.VMEM((group, 3, rows, LANES), f32),
        pltpu.VMEM((n_gy, 3, rows, LANES), f32),
        pltpu.VMEM((n_gy, 2, rows, LANES), f32),
        pltpu.VMEM((group, 2, rows, LANES), f32),
        pltpu.VMEM((rows, width), f32),
        dma((7,)),
        dma((2 * CHUNKS,)), dma((2 * CHUNKS,)),
        dma((2,)), dma((2,)),
        dma((1,)), dma((1,)),
        dma((group,)), dma((n_gy,)),
        dma((n_gy,)), dma((group,)),
        pltpu.SemaphoreType.REGULAR,
    ]
    sizes = (n_gx, n_gy, n_gz, layers, rows, width, points, cols)
    advanced, fresh = pl.pallas_call(
        functools.partial(kernel, sizes),
        out_shape=(
            jax.ShapeDtypeStruct(velocity.shape, f32),
            jax.ShapeDtypeStruct(column_state.shape, f32),
        ),
        in_specs=[hbm_spec] * 5,
        out_specs=(vmem_spec, vmem_spec),
        scratch_shapes=scratch,
        compiler_params=pltpu.CompilerParams(
            collective_id=0, has_side_effects=True, vmem_limit_bytes=32 * 1024 * 1024
        ),
    )(*[pltpu.with_memory_space_constraint(a, pltpu.HBM) for a in (velocity, column_state, height_index, rotor_mask, thrust)])

    return pl.pallas_call(
        write_out,
        out_shape=(
            jax.ShapeDtypeStruct(velocity.shape, f32),
            jax.ShapeDtypeStruct(column_state.shape, f32),
        ),
        in_specs=(vmem_spec, vmem_spec),
        out_specs=(hbm_spec, hbm_spec),
        scratch_shapes=[dma((5,))],
        compiler_params=pltpu.CompilerParams(vmem_limit_bytes=8 * 1024 * 1024),
    )(
        pltpu.with_memory_space_constraint(advanced, pltpu.VMEM),
        pltpu.with_memory_space_constraint(fresh, pltpu.VMEM),
    )


def solution(mesh):
    in_specs = (
        P(None, "gz", "gx", "gy"),
        P(None, None, "gx", ("gy", "gz")),
        P("gx", "gy"),
        P("gz", "gx", "gy"),
        P(),
    )
    out_specs = (P(None, "gz", "gx", "gy"), P(None, None, "gx", ("gy", "gz")))
    run = functools.partial(local, mesh.shape["gx"], mesh.shape["gy"], mesh.shape["gz"])
    return jax.shard_map(run, mesh=mesh, in_specs=in_specs, out_specs=out_specs, check_vma=False)
```

```python
import functools
import math

import jax
import jax.numpy as jnp
import numpy as np
from jax import lax
from jax.experimental import pallas as pl
from jax.experimental.pallas import tpu as pltpu
from jax.sharding import PartitionSpec as P

LEVELS = 8
LANES = 128
MESH = pl.DeviceIdType.MESH
CHUNKS = 4

time_step = 0.1
viscosity = 0.02
smag_coeff = 0.0289
karman = 0.41
wall_step = 0.05
stretch = 3.0


def column_constants(points):
    ladder = np.arange(points, dtype=np.float64) / (points - 1)
    spacing = (np.exp(stretch * ladder) - 1.0) / (math.exp(stretch) - 1.0)
    gap = spacing[1:] - spacing[:-1]
    middle = 0.5 * (spacing[1:] + spacing[:-1])
    laminar = viscosity / gap
    eddy = (karman * middle / gap) ** 2
    volume = np.zeros_like(gap)
    volume[1:] = 0.5 * (gap[1:] + gap[:-1]) / wall_step
    return [[float(np.float32(v)) for v in row] for row in (laminar, eddy, volume)]


def kernel(
    sizes,
    v_hbm, s_hbm, h_hbm, m_hbm, t_hbm,
    adv_ref, fresh_ref,
    v, s, h, mask, thrust_ref, tab_ref, eddy, coef_e, coef_f,
    xlo, xhi, zhalo, ypack_lo, ypack_hi, ylo, yhi,
    stage, tops, back, walls, push,
    load_sem, x_send, x_recv, y_send, y_recv, z_send, z_recv, t_send, t_recv, w_send, w_recv, ready,
):
    n_gx, n_gy, n_gz, layers, rows, width, points, cols = sizes
    group = n_gy * n_gz
    block = width // group
    tiles = width // LANES
    gx, gy, gz = lax.axis_index("gx"), lax.axis_index("gy"), lax.axis_index("gz")
    me = gy * n_gz + gz
    left, right = lax.rem(gx + n_gx - 1, n_gx), lax.rem(gx + 1, n_gx)
    below, above = lax.rem(gy + n_gy - 1, n_gy), lax.rem(gy + 1, n_gy)
    at_wall = gz == 0

    loads = [
        pltpu.make_async_copy(h_hbm, h, load_sem.at[0]),
        pltpu.make_async_copy(
            v_hbm.at[pl.ds(0, 2), pl.ds(0, LEVELS + 1)], v.at[pl.ds(0, 2), pl.ds(0, LEVELS + 1)], load_sem.at[1]
        ),
        pltpu.make_async_copy(
            v_hbm.at[pl.ds(0, 2), pl.ds(LEVELS + 1, layers - LEVELS - 1)],
            v.at[pl.ds(0, 2), pl.ds(LEVELS + 1, layers - LEVELS - 1)],
            load_sem.at[2],
        ),
        pltpu.make_async_copy(v_hbm.at[2], v.at[2], load_sem.at[3]),
        pltpu.make_async_copy(s_hbm, s, load_sem.at[4]),
        pltpu.make_async_copy(m_hbm.at[pl.ds(2, 8)], mask, load_sem.at[5]),
        pltpu.make_async_copy(t_hbm, thrust_ref, load_sem.at[6]),
    ]
    for load in loads:
        load.start()

    first = gx == 0

    def is_lead(x, y, z):
        return (y == 0) & (z == 0) & ((x == 1) | (x == n_gx - 1))

    lead = is_lead(gx, gy, gz)
    plain = jnp.logical_not(first | lead)
    mates = [(gx, r // n_gz, r % n_gz) for r in [lax.rem(me + d, group) for d in range(1, group)]]
    barrier = pltpu.get_barrier_semaphore()

    def tell(semaphore, device):
        pl.semaphore_signal(semaphore, inc=1, device_id=device, device_id_type=MESH)

    for side in (left, right):

        @pl.when((side != 0) & (first | jnp.logical_not(is_lead(side, gy, gz))))
        def _():
            tell(barrier, (side, gy, gz))

    for mate in mates:

        @pl.when(jnp.logical_not(is_lead(*mate)))
        def _():
            tell(barrier, mate)

    def x_copies(k):
        depth = layers // CHUNKS
        zs = pl.ds((CHUNKS - 1 - k) * depth, depth)
        to_right = pltpu.make_async_remote_copy(
            src_ref=v_hbm.at[:, zs, pl.ds(rows - 1, 1)], dst_ref=xlo.at[:, zs],
            send_sem=x_send.at[2 * k], recv_sem=x_recv.at[2 * k],
            device_id=(right, gy, gz), device_id_type=MESH,
        )
        to_left = pltpu.make_async_remote_copy(
            src_ref=v_hbm.at[:, zs, pl.ds(0, 1)], dst_ref=xhi.at[:, zs],
            send_sem=x_send.at[2 * k + 1], recv_sem=x_recv.at[2 * k + 1],
            device_id=(left, gy, gz), device_id_type=MESH,
        )
        return to_right, to_left

    @pl.when(lead)
    def _():
        pl.semaphore_wait(barrier, 1)
        for way, side in ((0, right), (1, left)):

            @pl.when(side == 0)
            def _():
                tell(ready, (side, gy, gz))
                for k in range(CHUNKS):
                    x_copies(k)[way].start()

    for j, entries in enumerate(column_constants(points)):
        for i, entry in enumerate(entries):
            tab_ref[j, i] = entry

    loads[0].wait()
    loads[1].wait()

    @pl.when(at_wall)
    def _():
        height = h[...]
        for c in range(2):
            picked = v[c, LEVELS]
            for level in range(1, LEVELS):
                picked = jnp.where(height == level, v[c, level], picked)
            for r in range(group):
                j, off = (r * block) // LANES, (r * block) % LANES
                part = picked[:, j * LANES : (j + 1) * LANES]
                if off:
                    part = pltpu.roll(part, LANES - off, 1)
                stage[r, c] = part
        sample_height = height.astype(jnp.float32) + 0.5
        for r in range(group):
            j, off = (r * block) // LANES, (r * block) % LANES
            part = sample_height[:, j * LANES : (j + 1) * LANES]
            if off:
                part = pltpu.roll(part, LANES - off, 1)
            stage[r, 2] = part
        tops[gy] = stage[me]

    @pl.when(first)
    def _():
        pl.semaphore_wait(barrier, group - 1)

    @pl.when(lead)
    def _():
        pl.semaphore_wait(ready, group)

    @pl.when(plain)
    def _():
        pl.semaphore_wait(barrier, group + 1)
        for side in (left, right):

            @pl.when((side == 0) | is_lead(side, gy, gz))
            def _():
                tell(ready, (side, gy, gz))

        for mate in mates:

            @pl.when(is_lead(*mate))
            def _():
                tell(ready, mate)

    def top_send(d):
        r = lax.rem(me + d, group)
        return pltpu.make_async_remote_copy(
            src_ref=stage.at[r], dst_ref=tops.at[gy], send_sem=t_send.at[d], recv_sem=t_recv.at[gy],
            device_id=(gx, r // n_gz, r % n_gz), device_id_type=MESH,
        )

    @pl.when(at_wall)
    def _():
        for d in range(1, group):
            top_send(d).start()

    @pl.when(lead)
    def _():
        for way, side in ((0, right), (1, left)):

            @pl.when(side != 0)
            def _():
                for k in range(CHUNKS):
                    x_copies(k)[way].start()

    @pl.when(plain)
    def _():
        for k in range(CHUNKS):
            for copy in x_copies(k):
                copy.start()

    edge = (layers - 1) * (1 - gz)
    z_copy = pltpu.make_async_remote_copy(
        src_ref=v_hbm.at[:, edge], dst_ref=zhalo, send_sem=z_send.at[0], recv_sem=z_recv.at[0],
        device_id=(gx, gy, 1 - gz), device_id_type=MESH,
    )
    z_copy.start()

    loads[2].wait()
    loads[3].wait()
    lane = lax.broadcasted_iota(jnp.int32, (rows, LANES), 1)

    def pack(k, carry):
        low, high = carry
        c, z = k // layers, k % layers
        low = jnp.where(lane == k, pltpu.roll(v[c, z, :, :LANES], k, 1), low)
        high = jnp.where(lane == k, pltpu.roll(v[c, z, :, width - LANES :], k + 1, 1), high)
        return low, high

    zeros = jnp.zeros((rows, LANES), jnp.float32)
    low, high = lax.fori_loop(0, 3 * layers, pack, (zeros, zeros), unroll=4)
    ypack_lo[...] = low
    ypack_hi[...] = high
    y_copies = [
        pltpu.make_async_remote_copy(
            src_ref=ypack_hi, dst_ref=ylo, send_sem=y_send.at[0], recv_sem=y_recv.at[0],
            device_id=(gx, above, gz), device_id_type=MESH,
        ),
        pltpu.make_async_remote_copy(
            src_ref=ypack_lo, dst_ref=yhi, send_sem=y_send.at[1], recv_sem=y_recv.at[1],
            device_id=(gx, below, gz), device_id_type=MESH,
        ),
    ]
    for copy in y_copies:
        copy.start()

    loads[4].wait()

    def shear(i, carry):
        du = s[0, i + 1] - s[0, i]
        dv = s[1, i + 1] - s[1, i]
        eddy[i] = tab_ref[1, i] * jnp.sqrt(du * du + dv * dv + 1e-06)
        return carry

    lax.fori_loop(0, points - 1, shear, 0, unroll=3)

    def top_wait(src):
        pltpu.make_async_remote_copy(
            src_ref=stage.at[0], dst_ref=tops.at[src], send_sem=t_send.at[0], recv_sem=t_recv.at[src],
            device_id=(gx, gy, 1 - gz), device_id_type=MESH,
        ).wait_recv()

    for src in range(n_gy):

        @pl.when(me != src * n_gz)
        def _():
            top_wait(src)

    lane_wide = lax.broadcasted_iota(jnp.int32, (rows, cols), 1)
    halves = cols // LANES

    def interleave(field):
        parts = []
        for half in range(halves):
            source = (lane + half * LANES) // n_gy
            owner = (lane + half * LANES) % n_gy
            out = None
            for src in range(n_gy):
                got = jnp.take_along_axis(tops[src, field], source, axis=1, mode="promise_in_bounds")
                out = got if out is None else jnp.where(owner == src, got, out)
            parts.append(out)
        return jnp.concatenate(parts, axis=1)

    top_u, top_v, height = interleave(0), interleave(1), interleave(2)
    inv_height = 1.0 / height

    last = points - 1
    fresh_ref[0, last] = top_u
    fresh_ref[1, last] = top_v
    fresh_ref[0, 0] = jnp.zeros_like(top_u)
    fresh_ref[1, 0] = jnp.zeros_like(top_u)

    def eliminate(k, carry):
        share, cond, f_u, f_v = carry
        i = last - 1 - k
        cond_low = tab_ref[0, i - 1] * inv_height + eddy[i - 1]
        volume = tab_ref[2, i] * height
        held = volume + share
        inverse = 1.0 / (held + cond_low)
        f_u = (volume * s[0, i] + cond * f_u) * inverse
        f_v = (volume * s[1, i] + cond * f_v) * inverse
        coef_e[i] = cond_low * inverse
        coef_f[0, i] = f_u
        coef_f[1, i] = f_v
        return cond_low * (held * inverse), cond_low, f_u, f_v

    cond_top = tab_ref[0, last - 1] * inv_height + eddy[last - 1]
    _, cond, f_u, f_v = lax.fori_loop(0, points - 2, eliminate, (cond_top, cond_top, top_u, top_v), unroll=2)
    stress = (cond * f_u, cond * f_v)

    for src in range(n_gy):
        index = lane * n_gy + src
        index = jnp.where(index < cols, index, 0)
        for c in range(2):
            out = None
            for half in range(halves):
                got = jnp.take_along_axis(
                    stress[c][:, half * LANES : (half + 1) * LANES], index % LANES, axis=1, mode="promise_in_bounds"
                )
                out = got if out is None else jnp.where(index // LANES == half, got, out)
            back[src, c] = out

    def wall_send(src):
        return pltpu.make_async_remote_copy(
            src_ref=back.at[src], dst_ref=walls.at[me], send_sem=w_send.at[src], recv_sem=w_recv.at[me],
            device_id=(gx, src, 0), device_id_type=MESH,
        )

    for src in range(n_gy):

        @pl.when(me != src * n_gz)
        def _():
            wall_send(src).start()

    @pl.when(at_wall)
    def _():
        walls[me] = back[gy]

    @pl.when(first)
    def _():
        pl.semaphore_wait(ready, 2)
        for k in range(CHUNKS):
            for copy in x_copies(k):
                copy.start()

    def substitute(k, carry):
        u, w = carry
        i = k + 1
        e = coef_e[i]
        u = e * u + coef_f[0, i]
        w = e * w + coef_f[1, i]
        fresh_ref[0, i] = u
        fresh_ref[1, i] = w
        return u, w

    zero = jnp.zeros_like(top_u)
    lax.fori_loop(0, points - 2, substitute, (zero, zero), unroll=2)

    for copy in y_copies:
        copy.wait_recv()
    z_copy.wait_recv()
    loads[5].wait()
    loads[6].wait()

    disks = mask[0]
    for k in range(1, 8):
        disks = jnp.maximum(disks, mask[k])
    force = jnp.zeros((rows, width), jnp.float32)
    for k in range(8):
        force = force + jnp.where(disks == k + 1, thrust_ref[k], 0.0)
    force = force * time_step
    for z in range(layers):
        if 2 <= z < 10:
            push[z] = jnp.where(jnp.logical_and(mask[z - 2] != 0, at_wall), force, 0.0)
        else:
            push[z] = jnp.zeros_like(force)

    row = lax.broadcasted_iota(jnp.int32, (rows, width), 0)
    col = lax.broadcasted_iota(jnp.int32, (rows, width), 1)

    def layer(z, below_v, above_v, wall):
        vel, xn, xp, yn, yp = [], [], [], [], []
        for c in range(3):
            here = v[c, z]
            vel.append(here)
            xp.append(jnp.where(row == 0, xlo[c, z], pltpu.roll(here, 1, 0)))
            xn.append(jnp.where(row == rows - 1, xhi[c, z], pltpu.roll(here, rows - 1, 0)))
            slot = c * layers + z
            low = pltpu.roll(ylo[...], LANES - slot, 1)
            high = pltpu.roll(yhi[...], LANES - 1 - slot, 1)
            low = jnp.concatenate([low] * tiles, axis=1)
            high = jnp.concatenate([high] * tiles, axis=1)
            yp.append(jnp.where(col == 0, low, pltpu.roll(here, 1, 1)))
            yn.append(jnp.where(col == width - 1, high, pltpu.roll(here, width - 1, 1)))
        zn, zp = above_v, below_v
        d_x = [xn[c] - xp[c] for c in range(3)]
        d_y = [yn[c] - yp[c] for c in range(3)]
        d_z = [zn[c] - zp[c] for c in range(3)]
        diag = d_x[0] * d_x[0] + d_y[1] * d_y[1] + d_z[2] * d_z[2]
        s_xy, s_xz, s_yz = d_y[0] + d_x[1], d_z[0] + d_x[2], d_z[1] + d_y[2]
        cross = s_xy * s_xy + s_xz * s_xz + s_yz * s_yz
        strain = jnp.sqrt(0.5 * diag + (0.25 * cross + 1e-06))
        viscous = time_step * viscosity + (time_step * smag_coeff) * strain
        for c in range(3):
            total = (xn[c] + xp[c]) + (yn[c] + yp[c]) + (zn[c] + zp[c])
            flux = (
                (xn[c] * xn[0] - xp[c] * xp[0]) + (yn[c] * yn[1] - yp[c] * yp[1]) + (zn[c] * zn[2] - zp[c] * zp[2])
            )
            lap = total - 6.0 * vel[c]
            if wall is not None and c < 2:
                lap = lap + wall[0] * vel[c]
            out = vel[c] + (viscous * lap - (0.5 * time_step) * flux)
            if wall is not None and c < 2:
                out = out - time_step * wall[1][c]
            if c == 2:
                out = out - push[z]
            adv_ref[c, z] = out

    def velocity_at(z):
        return [v[c, z] for c in range(3)]

    def x_wait(k):
        for copy in x_copies(k):
            copy.wait_recv()

    depth = layers // CHUNKS
    x_wait(0)
    bottom = at_wall.astype(jnp.float32)
    layer(layers - 1, velocity_at(layers - 2), [zhalo[c] * bottom for c in range(3)], None)

    def inner(z, carry):
        layer(z, velocity_at(z - 1), velocity_at(z + 1), None)
        return carry

    lax.fori_loop(max(layers - depth, 1), layers - 1, inner, 0)
    for k in range(1, CHUNKS):
        x_wait(k)
        low = (CHUNKS - 1 - k) * depth
        lax.fori_loop(max(low, 1), low + depth, inner, 0)

    def wall_wait(r):
        pltpu.make_async_remote_copy(
            src_ref=back.at[0], dst_ref=walls.at[r], send_sem=w_send.at[0], recv_sem=w_recv.at[r],
            device_id=(gx, gy, 1 - gz), device_id_type=MESH,
        ).wait_recv()

    @pl.when(at_wall)
    def _():
        for r in range(group):

            @pl.when(me != r)
            def _():
                wall_wait(r)

        wall = []
        for c in range(2):
            parts = []
            for j in range(tiles):
                out = None
                for r in range(group):
                    if (r * block) // LANES == j:
                        off = (r * block) % LANES
                        got = walls[r, c]
                        if off:
                            got = pltpu.roll(got, off, 1)
                        out = got if out is None else jnp.where(lane >= off, got, out)
                parts.append(out)
            wall.append(jnp.concatenate(parts, axis=1))
        layer(0, [jnp.zeros((rows, width), jnp.float32)] * 3, velocity_at(1), (1.0, wall))

    @pl.when(jnp.logical_not(at_wall))
    def _():
        layer(0, [zhalo[c] for c in range(3)], velocity_at(1), None)

    @pl.when(at_wall)
    def _():
        for d in range(1, group):
            top_send(d).wait_send()

    for src in range(n_gy):

        @pl.when(me != src * n_gz)
        def _():
            wall_send(src).wait_send()

    for k in range(CHUNKS):
        for copy in x_copies(k):
            copy.wait_send()
    for copy in y_copies:
        copy.wait_send()
    z_copy.wait_send()


def write_out(advanced, fresh, advanced_hbm, fresh_hbm, sem):
    copies = [pltpu.make_async_copy(fresh.at[c], fresh_hbm.at[c], sem.at[c]) for c in range(2)]
    copies += [pltpu.make_async_copy(advanced.at[c], advanced_hbm.at[c], sem.at[2 + c]) for c in range(3)]
    for copy in copies:
        copy.start()
    for copy in copies:
        copy.wait()


def local(n_gx, n_gy, n_gz, velocity, column_state, height_index, rotor_mask, thrust):
    _, layers, rows, width = velocity.shape
    _, points, _, cols = column_state.shape
    group = n_gy * n_gz
    hbm_spec = pl.BlockSpec(memory_space=pltpu.HBM)
    vmem_spec = pl.BlockSpec(memory_space=pltpu.VMEM)
    f32 = jnp.float32
    dma = pltpu.SemaphoreType.DMA
    scratch = [
        pltpu.VMEM(velocity.shape, f32),
        pltpu.VMEM(column_state.shape, f32),
        pltpu.VMEM(height_index.shape, jnp.int32),
        pltpu.VMEM((8, rows, width), jnp.int32),
        pltpu.SMEM(thrust.shape, f32),
        pltpu.SMEM((3, points - 1), f32),
        pltpu.VMEM((points - 1, rows, cols), f32),
        pltpu.VMEM((points - 1, rows, cols), f32),
        pltpu.VMEM((2, points - 1, rows, cols), f32),
        pltpu.VMEM((3, layers, 1, width), f32),
        pltpu.VMEM((3, layers, 1, width), f32),
        pltpu.VMEM((3, rows, width), f32),
        pltpu.VMEM((rows, LANES), f32),
        pltpu.VMEM((rows, LANES), f32),
        pltpu.VMEM((rows, LANES), f32),
        pltpu.VMEM((rows, LANES), f32),
        pltpu.VMEM((group, 3, rows, LANES), f32),
        pltpu.VMEM((n_gy, 3, rows, LANES), f32),
        pltpu.VMEM((n_gy, 2, rows, LANES), f32),
        pltpu.VMEM((group, 2, rows, LANES), f32),
        pltpu.VMEM((layers, rows, width), f32),
        dma((7,)),
        dma((2 * CHUNKS,)), dma((2 * CHUNKS,)),
        dma((2,)), dma((2,)),
        dma((1,)), dma((1,)),
        dma((group,)), dma((n_gy,)),
        dma((n_gy,)), dma((group,)),
        pltpu.SemaphoreType.REGULAR,
    ]
    sizes = (n_gx, n_gy, n_gz, layers, rows, width, points, cols)
    advanced, fresh = pl.pallas_call(
        functools.partial(kernel, sizes),
        out_shape=(
            jax.ShapeDtypeStruct(velocity.shape, f32),
            jax.ShapeDtypeStruct(column_state.shape, f32),
        ),
        in_specs=[hbm_spec] * 5,
        out_specs=(vmem_spec, vmem_spec),
        scratch_shapes=scratch,
        compiler_params=pltpu.CompilerParams(
            collective_id=0, has_side_effects=True, vmem_limit_bytes=32 * 1024 * 1024
        ),
    )(*[pltpu.with_memory_space_constraint(a, pltpu.HBM) for a in (velocity, column_state, height_index, rotor_mask, thrust)])

    return pl.pallas_call(
        write_out,
        out_shape=(
            jax.ShapeDtypeStruct(velocity.shape, f32),
            jax.ShapeDtypeStruct(column_state.shape, f32),
        ),
        in_specs=(vmem_spec, vmem_spec),
        out_specs=(hbm_spec, hbm_spec),
        scratch_shapes=[dma((5,))],
        compiler_params=pltpu.CompilerParams(vmem_limit_bytes=8 * 1024 * 1024),
    )(
        pltpu.with_memory_space_constraint(advanced, pltpu.VMEM),
        pltpu.with_memory_space_constraint(fresh, pltpu.VMEM),
    )


def solution(mesh):
    in_specs = (
        P(None, "gz", "gx", "gy"),
        P(None, None, "gx", ("gy", "gz")),
        P("gx", "gy"),
        P("gz", "gx", "gy"),
        P(),
    )
    out_specs = (P(None, "gz", "gx", "gy"), P(None, None, "gx", ("gy", "gz")))
    run = functools.partial(local, mesh.shape["gx"], mesh.shape["gy"], mesh.shape["gz"])
    return jax.shard_map(run, mesh=mesh, in_specs=in_specs, out_specs=out_specs, check_vma=False)
```

```python
import functools
import math

import jax
import jax.numpy as jnp
import numpy as np
from jax import lax
from jax.experimental import pallas as pl
from jax.experimental.pallas import tpu as pltpu
from jax.sharding import PartitionSpec as P

LEVELS = 8
LANES = 128
MESH = pl.DeviceIdType.MESH
CHUNKS = 4

time_step = 0.1
viscosity = 0.02
smag_coeff = 0.0289
karman = 0.41
wall_step = 0.05
stretch = 3.0


def column_constants(points):
    ladder = np.arange(points, dtype=np.float64) / (points - 1)
    spacing = (np.exp(stretch * ladder) - 1.0) / (math.exp(stretch) - 1.0)
    gap = spacing[1:] - spacing[:-1]
    middle = 0.5 * (spacing[1:] + spacing[:-1])
    laminar = viscosity / gap
    eddy = (karman * middle / gap) ** 2
    volume = np.zeros_like(gap)
    volume[1:] = 0.5 * (gap[1:] + gap[:-1]) / wall_step
    return [[float(np.float32(v)) for v in row] for row in (laminar, eddy, volume)]


def kernel(
    sizes,
    v_hbm, s_hbm, h_hbm, m_hbm, t_hbm,
    adv_ref, fresh_ref,
    v, s, h, mask, thrust_ref, tab_ref, eddy, coef_e, coef_f,
    xlo, xhi, zhalo, ypack_lo, ypack_hi, ylo, yhi,
    stage, tops, back, walls, push,
    load_sem, x_send, x_recv, y_send, y_recv, z_send, z_recv, t_send, t_recv, w_send, w_recv, ready,
):
    n_gx, n_gy, n_gz, layers, rows, width, points, cols = sizes
    group = n_gy * n_gz
    block = width // group
    tiles = width // LANES
    gx, gy, gz = lax.axis_index("gx"), lax.axis_index("gy"), lax.axis_index("gz")
    me = gy * n_gz + gz
    left, right = lax.rem(gx + n_gx - 1, n_gx), lax.rem(gx + 1, n_gx)
    below, above = lax.rem(gy + n_gy - 1, n_gy), lax.rem(gy + 1, n_gy)
    at_wall = gz == 0

    loads = [
        pltpu.make_async_copy(h_hbm, h, load_sem.at[0]),
        pltpu.make_async_copy(
            v_hbm.at[pl.ds(0, 2), pl.ds(0, LEVELS + 1)], v.at[pl.ds(0, 2), pl.ds(0, LEVELS + 1)], load_sem.at[1]
        ),
        pltpu.make_async_copy(
            v_hbm.at[pl.ds(0, 2), pl.ds(LEVELS + 1, layers - LEVELS - 1)],
            v.at[pl.ds(0, 2), pl.ds(LEVELS + 1, layers - LEVELS - 1)],
            load_sem.at[2],
        ),
        pltpu.make_async_copy(v_hbm.at[2], v.at[2], load_sem.at[3]),
        pltpu.make_async_copy(s_hbm, s, load_sem.at[4]),
        pltpu.make_async_copy(m_hbm.at[pl.ds(2, 8)], mask, load_sem.at[5]),
        pltpu.make_async_copy(t_hbm, thrust_ref, load_sem.at[6]),
    ]
    for load in loads:
        load.start()

    first = gx == 0

    def is_lead(x, y, z):
        return (y == 0) & ((x == 1) | (x == n_gx - 1))

    lead = is_lead(gx, gy, gz)
    plain = jnp.logical_not(first | lead)
    mates = [(gx, r // n_gz, r % n_gz) for r in [lax.rem(me + d, group) for d in range(1, group)]]
    barrier = pltpu.get_barrier_semaphore()

    def tell(semaphore, device):
        pl.semaphore_signal(semaphore, inc=1, device_id=device, device_id_type=MESH)

    for side in (left, right):

        @pl.when((side != 0) & (first | jnp.logical_not(is_lead(side, gy, gz))))
        def _():
            tell(barrier, (side, gy, gz))

    for mate in mates:

        @pl.when(jnp.logical_not(is_lead(*mate)))
        def _():
            tell(barrier, mate)

    def x_copies(k):
        depth = layers // CHUNKS
        zs = pl.ds((CHUNKS - 1 - k) * depth, depth)
        to_right = pltpu.make_async_remote_copy(
            src_ref=v_hbm.at[:, zs, pl.ds(rows - 1, 1)], dst_ref=xlo.at[:, zs],
            send_sem=x_send.at[2 * k], recv_sem=x_recv.at[2 * k],
            device_id=(right, gy, gz), device_id_type=MESH,
        )
        to_left = pltpu.make_async_remote_copy(
            src_ref=v_hbm.at[:, zs, pl.ds(0, 1)], dst_ref=xhi.at[:, zs],
            send_sem=x_send.at[2 * k + 1], recv_sem=x_recv.at[2 * k + 1],
            device_id=(left, gy, gz), device_id_type=MESH,
        )
        return to_right, to_left

    @pl.when(lead)
    def _():
        pl.semaphore_wait(barrier, 1)
        for way, side in ((0, right), (1, left)):

            @pl.when(side == 0)
            def _():
                tell(ready, (side, gy, gz))
                for k in range(CHUNKS):
                    x_copies(k)[way].start()

    for j, entries in enumerate(column_constants(points)):
        for i, entry in enumerate(entries):
            tab_ref[j, i] = entry

    loads[0].wait()
    loads[1].wait()

    @pl.when(at_wall)
    def _():
        height = h[...]
        for c in range(2):
            picked = v[c, LEVELS]
            for level in range(1, LEVELS):
                picked = jnp.where(height == level, v[c, level], picked)
            for r in range(group):
                j, off = (r * block) // LANES, (r * block) % LANES
                part = picked[:, j * LANES : (j + 1) * LANES]
                if off:
                    part = pltpu.roll(part, LANES - off, 1)
                stage[r, c] = part
        sample_height = height.astype(jnp.float32) + 0.5
        for r in range(group):
            j, off = (r * block) // LANES, (r * block) % LANES
            part = sample_height[:, j * LANES : (j + 1) * LANES]
            if off:
                part = pltpu.roll(part, LANES - off, 1)
            stage[r, 2] = part
        tops[gy] = stage[me]

    @pl.when(first)
    def _():
        pl.semaphore_wait(barrier, group - 1)

    @pl.when(lead)
    def _():
        pl.semaphore_wait(ready, group - n_gz + 1)

    @pl.when(plain)
    def _():
        pl.semaphore_wait(barrier, group + 1)
        for side in (left, right):

            @pl.when((side == 0) | is_lead(side, gy, gz))
            def _():
                tell(ready, (side, gy, gz))

        for mate in mates:

            @pl.when(is_lead(*mate))
            def _():
                tell(ready, mate)

    def top_send(d):
        r = lax.rem(me + d, group)
        return pltpu.make_async_remote_copy(
            src_ref=stage.at[r], dst_ref=tops.at[gy], send_sem=t_send.at[d], recv_sem=t_recv.at[gy],
            device_id=(gx, r // n_gz, r % n_gz), device_id_type=MESH,
        )

    @pl.when(at_wall)
    def _():
        for d in range(1, group):
            top_send(d).start()

    @pl.when(lead)
    def _():
        for way, side in ((0, right), (1, left)):

            @pl.when(side != 0)
            def _():
                for k in range(CHUNKS):
                    x_copies(k)[way].start()

    @pl.when(plain)
    def _():
        for k in range(CHUNKS):
            for copy in x_copies(k):
                copy.start()

    edge = (layers - 1) * (1 - gz)
    z_copy = pltpu.make_async_remote_copy(
        src_ref=v_hbm.at[:, edge], dst_ref=zhalo, send_sem=z_send.at[0], recv_sem=z_recv.at[0],
        device_id=(gx, gy, 1 - gz), device_id_type=MESH,
    )
    z_copy.start()

    loads[2].wait()
    loads[3].wait()
    lane = lax.broadcasted_iota(jnp.int32, (rows, LANES), 1)

    def pack(k, carry):
        low, high = carry
        c, z = k // layers, k % layers
        low = jnp.where(lane == k, pltpu.roll(v[c, z, :, :LANES], k, 1), low)
        high = jnp.where(lane == k, pltpu.roll(v[c, z, :, width - LANES :], k + 1, 1), high)
        return low, high

    zeros = jnp.zeros((rows, LANES), jnp.float32)
    low, high = lax.fori_loop(0, 3 * layers, pack, (zeros, zeros), unroll=4)
    ypack_lo[...] = low
    ypack_hi[...] = high
    y_copies = [
        pltpu.make_async_remote_copy(
            src_ref=ypack_hi, dst_ref=ylo, send_sem=y_send.at[0], recv_sem=y_recv.at[0],
            device_id=(gx, above, gz), device_id_type=MESH,
        ),
        pltpu.make_async_remote_copy(
            src_ref=ypack_lo, dst_ref=yhi, send_sem=y_send.at[1], recv_sem=y_recv.at[1],
            device_id=(gx, below, gz), device_id_type=MESH,
        ),
    ]
    for copy in y_copies:
        copy.start()

    loads[4].wait()

    def shear(i, carry):
        du = s[0, i + 1] - s[0, i]
        dv = s[1, i + 1] - s[1, i]
        eddy[i] = tab_ref[1, i] * jnp.sqrt(du * du + dv * dv + 1e-06)
        return carry

    lax.fori_loop(0, points - 1, shear, 0, unroll=3)

    def top_wait(src):
        pltpu.make_async_remote_copy(
            src_ref=stage.at[0], dst_ref=tops.at[src], send_sem=t_send.at[0], recv_sem=t_recv.at[src],
            device_id=(gx, gy, 1 - gz), device_id_type=MESH,
        ).wait_recv()

    for src in range(n_gy):

        @pl.when(me != src * n_gz)
        def _():
            top_wait(src)

    def answer(now):
        @pl.when(first & now)
        def _():
            pl.semaphore_wait(ready, 2)
            for k in range(CHUNKS):
                for copy in x_copies(k):
                    copy.start()

    answer(gy == 0)
    halves = cols // LANES

    def interleave(field):
        parts = []
        for half in range(halves):
            source = (lane + half * LANES) // n_gy
            owner = (lane + half * LANES) % n_gy
            out = None
            for src in range(n_gy):
                got = jnp.take_along_axis(tops[src, field], source, axis=1, mode="promise_in_bounds")
                out = got if out is None else jnp.where(owner == src, got, out)
            parts.append(out)
        return jnp.concatenate(parts, axis=1)

    top_u, top_v, height = interleave(0), interleave(1), interleave(2)
    inv_height = 1.0 / height

    last = points - 1
    fresh_ref[0, last] = top_u
    fresh_ref[1, last] = top_v
    fresh_ref[0, 0] = jnp.zeros_like(top_u)
    fresh_ref[1, 0] = jnp.zeros_like(top_u)

    def eliminate(k, carry):
        share, cond, f_u, f_v = carry
        i = last - 1 - k
        cond_low = tab_ref[0, i - 1] * inv_height + eddy[i - 1]
        volume = tab_ref[2, i] * height
        held = volume + share
        inverse = 1.0 / (held + cond_low)
        f_u = (volume * s[0, i] + cond * f_u) * inverse
        f_v = (volume * s[1, i] + cond * f_v) * inverse
        coef_e[i] = cond_low * inverse
        coef_f[0, i] = f_u
        coef_f[1, i] = f_v
        return cond_low * (held * inverse), cond_low, f_u, f_v

    cond_top = tab_ref[0, last - 1] * inv_height + eddy[last - 1]
    _, cond, f_u, f_v = lax.fori_loop(0, points - 2, eliminate, (cond_top, cond_top, top_u, top_v), unroll=2)
    stress = (cond * f_u, cond * f_v)

    for src in range(n_gy):
        index = lane * n_gy + src
        index = jnp.where(index < cols, index, 0)
        for c in range(2):
            out = None
            for half in range(halves):
                got = jnp.take_along_axis(
                    stress[c][:, half * LANES : (half + 1) * LANES], index % LANES, axis=1, mode="promise_in_bounds"
                )
                out = got if out is None else jnp.where(index // LANES == half, got, out)
            back[src, c] = out

    def wall_send(src):
        return pltpu.make_async_remote_copy(
            src_ref=back.at[src], dst_ref=walls.at[me], send_sem=w_send.at[src], recv_sem=w_recv.at[me],
            device_id=(gx, src, 0), device_id_type=MESH,
        )

    for src in range(n_gy):

        @pl.when(me != src * n_gz)
        def _():
            wall_send(src).start()

    @pl.when(at_wall)
    def _():
        walls[me] = back[gy]

    answer(gy != 0)

    def substitute(k, carry):
        u, w = carry
        i = k + 1
        e = coef_e[i]
        u = e * u + coef_f[0, i]
        w = e * w + coef_f[1, i]
        fresh_ref[0, i] = u
        fresh_ref[1, i] = w
        return u, w

    zero = jnp.zeros_like(top_u)
    lax.fori_loop(0, points - 2, substitute, (zero, zero), unroll=2)

    for copy in y_copies:
        copy.wait_recv()
    z_copy.wait_recv()
    loads[5].wait()
    loads[6].wait()

    disks = mask[0]
    for k in range(1, 8):
        disks = jnp.maximum(disks, mask[k])
    force = jnp.zeros((rows, width), jnp.float32)
    for k in range(8):
        force = force + jnp.where(disks == k + 1, thrust_ref[k], 0.0)
    force = force * time_step
    for z in range(layers):
        if 2 <= z < 10:
            push[z] = jnp.where(jnp.logical_and(mask[z - 2] != 0, at_wall), force, 0.0)
        else:
            push[z] = jnp.zeros_like(force)

    row = lax.broadcasted_iota(jnp.int32, (rows, width), 0)
    col = lax.broadcasted_iota(jnp.int32, (rows, width), 1)

    def layer(z, below_v, above_v, wall):
        vel, xn, xp, yn, yp = [], [], [], [], []
        for c in range(3):
            here = v[c, z]
            vel.append(here)
            xp.append(jnp.where(row == 0, xlo[c, z], pltpu.roll(here, 1, 0)))
            xn.append(jnp.where(row == rows - 1, xhi[c, z], pltpu.roll(here, rows - 1, 0)))
            slot = c * layers + z
            low = pltpu.roll(ylo[...], LANES - slot, 1)
            high = pltpu.roll(yhi[...], LANES - 1 - slot, 1)
            low = jnp.concatenate([low] * tiles, axis=1)
            high = jnp.concatenate([high] * tiles, axis=1)
            yp.append(jnp.where(col == 0, low, pltpu.roll(here, 1, 1)))
            yn.append(jnp.where(col == width - 1, high, pltpu.roll(here, width - 1, 1)))
        zn, zp = above_v, below_v
        d_x = [xn[c] - xp[c] for c in range(3)]
        d_y = [yn[c] - yp[c] for c in range(3)]
        d_z = [zn[c] - zp[c] for c in range(3)]
        diag = d_x[0] * d_x[0] + d_y[1] * d_y[1] + d_z[2] * d_z[2]
        s_xy, s_xz, s_yz = d_y[0] + d_x[1], d_z[0] + d_x[2], d_z[1] + d_y[2]
        cross = s_xy * s_xy + s_xz * s_xz + s_yz * s_yz
        strain = jnp.sqrt(0.5 * diag + (0.25 * cross + 1e-06))
        viscous = time_step * viscosity + (time_step * smag_coeff) * strain
        for c in range(3):
            total = (xn[c] + xp[c]) + (yn[c] + yp[c]) + (zn[c] + zp[c])
            flux = (
                (xn[c] * xn[0] - xp[c] * xp[0]) + (yn[c] * yn[1] - yp[c] * yp[1]) + (zn[c] * zn[2] - zp[c] * zp[2])
            )
            lap = total - 6.0 * vel[c]
            if wall is not None and c < 2:
                lap = lap + wall[0] * vel[c]
            out = vel[c] + (viscous * lap - (0.5 * time_step) * flux)
            if wall is not None and c < 2:
                out = out - time_step * wall[1][c]
            if c == 2:
                out = out - push[z]
            adv_ref[c, z] = out

    def velocity_at(z):
        return [v[c, z] for c in range(3)]

    def x_wait(k):
        for copy in x_copies(k):
            copy.wait_recv()

    depth = layers // CHUNKS
    x_wait(0)
    bottom = at_wall.astype(jnp.float32)
    layer(layers - 1, velocity_at(layers - 2), [zhalo[c] * bottom for c in range(3)], None)

    def inner(z, carry):
        layer(z, velocity_at(z - 1), velocity_at(z + 1), None)
        return carry

    lax.fori_loop(max(layers - depth, 1), layers - 1, inner, 0)
    for k in range(1, CHUNKS):
        x_wait(k)
        low = (CHUNKS - 1 - k) * depth
        lax.fori_loop(max(low, 1), low + depth, inner, 0)

    def wall_wait(r):
        pltpu.make_async_remote_copy(
            src_ref=back.at[0], dst_ref=walls.at[r], send_sem=w_send.at[0], recv_sem=w_recv.at[r],
            device_id=(gx, gy, 1 - gz), device_id_type=MESH,
        ).wait_recv()

    @pl.when(at_wall)
    def _():
        for r in range(group):

            @pl.when(me != r)
            def _():
                wall_wait(r)

        wall = []
        for c in range(2):
            parts = []
            for j in range(tiles):
                out = None
                for r in range(group):
                    if (r * block) // LANES == j:
                        off = (r * block) % LANES
                        got = walls[r, c]
                        if off:
                            got = pltpu.roll(got, off, 1)
                        out = got if out is None else jnp.where(lane >= off, got, out)
                parts.append(out)
            wall.append(jnp.concatenate(parts, axis=1))
        layer(0, [jnp.zeros((rows, width), jnp.float32)] * 3, velocity_at(1), (1.0, wall))

    @pl.when(jnp.logical_not(at_wall))
    def _():
        layer(0, [zhalo[c] for c in range(3)], velocity_at(1), None)

    @pl.when(at_wall)
    def _():
        for d in range(1, group):
            top_send(d).wait_send()

    for src in range(n_gy):

        @pl.when(me != src * n_gz)
        def _():
            wall_send(src).wait_send()

    for k in range(CHUNKS):
        for copy in x_copies(k):
            copy.wait_send()
    for copy in y_copies:
        copy.wait_send()
    z_copy.wait_send()


def write_out(advanced, fresh, advanced_hbm, fresh_hbm, sem):
    copies = [pltpu.make_async_copy(fresh.at[c], fresh_hbm.at[c], sem.at[c]) for c in range(2)]
    copies += [pltpu.make_async_copy(advanced.at[c], advanced_hbm.at[c], sem.at[2 + c]) for c in range(3)]
    for copy in copies:
        copy.start()
    for copy in copies:
        copy.wait()


def local(n_gx, n_gy, n_gz, velocity, column_state, height_index, rotor_mask, thrust):
    _, layers, rows, width = velocity.shape
    _, points, _, cols = column_state.shape
    group = n_gy * n_gz
    hbm_spec = pl.BlockSpec(memory_space=pltpu.HBM)
    vmem_spec = pl.BlockSpec(memory_space=pltpu.VMEM)
    f32 = jnp.float32
    dma = pltpu.SemaphoreType.DMA
    scratch = [
        pltpu.VMEM(velocity.shape, f32),
        pltpu.VMEM(column_state.shape, f32),
        pltpu.VMEM(height_index.shape, jnp.int32),
        pltpu.VMEM((8, rows, width), jnp.int32),
        pltpu.SMEM(thrust.shape, f32),
        pltpu.SMEM((3, points - 1), f32),
        pltpu.VMEM((points - 1, rows, cols), f32),
        pltpu.VMEM((points - 1, rows, cols), f32),
        pltpu.VMEM((2, points - 1, rows, cols), f32),
        pltpu.VMEM((3, layers, 1, width), f32),
        pltpu.VMEM((3, layers, 1, width), f32),
        pltpu.VMEM((3, rows, width), f32),
        pltpu.VMEM((rows, LANES), f32),
        pltpu.VMEM((rows, LANES), f32),
        pltpu.VMEM((rows, LANES), f32),
        pltpu.VMEM((rows, LANES), f32),
        pltpu.VMEM((group, 3, rows, LANES), f32),
        pltpu.VMEM((n_gy, 3, rows, LANES), f32),
        pltpu.VMEM((n_gy, 2, rows, LANES), f32),
        pltpu.VMEM((group, 2, rows, LANES), f32),
        pltpu.VMEM((layers, rows, width), f32),
        dma((7,)),
        dma((2 * CHUNKS,)), dma((2 * CHUNKS,)),
        dma((2,)), dma((2,)),
        dma((1,)), dma((1,)),
        dma((group,)), dma((n_gy,)),
        dma((n_gy,)), dma((group,)),
        pltpu.SemaphoreType.REGULAR,
    ]
    sizes = (n_gx, n_gy, n_gz, layers, rows, width, points, cols)
    advanced, fresh = pl.pallas_call(
        functools.partial(kernel, sizes),
        out_shape=(
            jax.ShapeDtypeStruct(velocity.shape, f32),
            jax.ShapeDtypeStruct(column_state.shape, f32),
        ),
        in_specs=[hbm_spec] * 5,
        out_specs=(vmem_spec, vmem_spec),
        scratch_shapes=scratch,
        compiler_params=pltpu.CompilerParams(
            collective_id=0, has_side_effects=True, vmem_limit_bytes=32 * 1024 * 1024
        ),
    )(*[pltpu.with_memory_space_constraint(a, pltpu.HBM) for a in (velocity, column_state, height_index, rotor_mask, thrust)])

    return pl.pallas_call(
        write_out,
        out_shape=(
            jax.ShapeDtypeStruct(velocity.shape, f32),
            jax.ShapeDtypeStruct(column_state.shape, f32),
        ),
        in_specs=(vmem_spec, vmem_spec),
        out_specs=(hbm_spec, hbm_spec),
        scratch_shapes=[dma((5,))],
        compiler_params=pltpu.CompilerParams(vmem_limit_bytes=8 * 1024 * 1024),
    )(
        pltpu.with_memory_space_constraint(advanced, pltpu.VMEM),
        pltpu.with_memory_space_constraint(fresh, pltpu.VMEM),
    )


def solution(mesh):
    in_specs = (
        P(None, "gz", "gx", "gy"),
        P(None, None, "gx", ("gy", "gz")),
        P("gx", "gy"),
        P("gz", "gx", "gy"),
        P(),
    )
    out_specs = (P(None, "gz", "gx", "gy"), P(None, None, "gx", ("gy", "gz")))
    run = functools.partial(local, mesh.shape["gx"], mesh.shape["gy"], mesh.shape["gz"])
    return jax.shard_map(run, mesh=mesh, in_specs=in_specs, out_specs=out_specs, check_vma=False)
```

```python
import functools
import math

import jax
import jax.numpy as jnp
import numpy as np
from jax import lax
from jax.experimental import pallas as pl
from jax.experimental.pallas import tpu as pltpu
from jax.sharding import PartitionSpec as P

LEVELS = 8
LANES = 128
MESH = pl.DeviceIdType.MESH
SIXTEENTHS = (16, 11, 6, 2, 0)
CHUNKS = len(SIXTEENTHS) - 1

time_step = 0.1
viscosity = 0.02
smag_coeff = 0.0289
karman = 0.41
wall_step = 0.05
stretch = 3.0


def column_constants(points):
    ladder = np.arange(points, dtype=np.float64) / (points - 1)
    spacing = (np.exp(stretch * ladder) - 1.0) / (math.exp(stretch) - 1.0)
    gap = spacing[1:] - spacing[:-1]
    middle = 0.5 * (spacing[1:] + spacing[:-1])
    laminar = viscosity / gap
    eddy = (karman * middle / gap) ** 2
    volume = np.zeros_like(gap)
    volume[1:] = 0.5 * (gap[1:] + gap[:-1]) / wall_step
    return [[float(np.float32(v)) for v in row] for row in (laminar, eddy, volume)]


def kernel(
    sizes,
    v_hbm, s_hbm, h_hbm, m_hbm, t_hbm,
    adv_ref, fresh_ref,
    v, s, h, mask, thrust_ref, tab_ref, eddy, coef_e, coef_f,
    xlo, xhi, zhalo, ypack_lo, ypack_hi, ylo, yhi,
    stage, tops, back, walls, push, part,
    load_sem, x_send, x_recv, y_send, y_recv, z_send, z_recv, t_send, t_recv, w_send, w_recv, ready,
):
    n_gx, n_gy, n_gz, layers, rows, width, points, cols = sizes
    group = n_gy * n_gz
    block = width // group
    tiles = width // LANES
    gx, gy, gz = lax.axis_index("gx"), lax.axis_index("gy"), lax.axis_index("gz")
    me = gy * n_gz + gz
    left, right = lax.rem(gx + n_gx - 1, n_gx), lax.rem(gx + 1, n_gx)
    below, above = lax.rem(gy + n_gy - 1, n_gy), lax.rem(gy + 1, n_gy)
    at_wall = gz == 0
    cuts = [layers * sixteenth // 16 for sixteenth in SIXTEENTHS]

    loads = [
        pltpu.make_async_copy(h_hbm, h, load_sem.at[0]),
        pltpu.make_async_copy(
            v_hbm.at[pl.ds(0, 2), pl.ds(0, LEVELS + 1)], v.at[pl.ds(0, 2), pl.ds(0, LEVELS + 1)], load_sem.at[1]
        ),
        pltpu.make_async_copy(
            v_hbm.at[pl.ds(0, 2), pl.ds(LEVELS + 1, layers - LEVELS - 1)],
            v.at[pl.ds(0, 2), pl.ds(LEVELS + 1, layers - LEVELS - 1)],
            load_sem.at[2],
        ),
        pltpu.make_async_copy(v_hbm.at[2], v.at[2], load_sem.at[3]),
        pltpu.make_async_copy(s_hbm, s, load_sem.at[4]),
        pltpu.make_async_copy(m_hbm.at[pl.ds(2, 8)], mask, load_sem.at[5]),
        pltpu.make_async_copy(t_hbm, thrust_ref, load_sem.at[6]),
    ]
    for load in loads:
        load.start()

    first = gx == 0

    def is_lead(x, y, z):
        return (y == 0) & ((x == 1) | (x == n_gx - 1))

    lead = is_lead(gx, gy, gz)
    plain = jnp.logical_not(first | lead)
    mates = [(gx, r // n_gz, r % n_gz) for r in [lax.rem(me + d, group) for d in range(1, group)]]
    barrier = pltpu.get_barrier_semaphore()

    def tell(semaphore, device):
        pl.semaphore_signal(semaphore, inc=1, device_id=device, device_id_type=MESH)

    for side in (left, right):

        @pl.when((side != 0) & (first | jnp.logical_not(is_lead(side, gy, gz))))
        def _():
            tell(barrier, (side, gy, gz))

    for mate in mates:

        @pl.when(jnp.logical_not(is_lead(*mate)))
        def _():
            tell(barrier, mate)

    def x_copies(k):
        zs = pl.ds(cuts[k + 1], cuts[k] - cuts[k + 1])
        to_right = pltpu.make_async_remote_copy(
            src_ref=v_hbm.at[:, zs, pl.ds(rows - 1, 1)], dst_ref=xlo.at[:, zs],
            send_sem=x_send.at[2 * k], recv_sem=x_recv.at[2 * k],
            device_id=(right, gy, gz), device_id_type=MESH,
        )
        to_left = pltpu.make_async_remote_copy(
            src_ref=v_hbm.at[:, zs, pl.ds(0, 1)], dst_ref=xhi.at[:, zs],
            send_sem=x_send.at[2 * k + 1], recv_sem=x_recv.at[2 * k + 1],
            device_id=(left, gy, gz), device_id_type=MESH,
        )
        return to_right, to_left

    @pl.when(lead)
    def _():
        pl.semaphore_wait(barrier, 1)
        for way, side in ((0, right), (1, left)):

            @pl.when(side == 0)
            def _():
                tell(ready, (side, gy, gz))
                for k in range(CHUNKS):
                    x_copies(k)[way].start()

    for j, entries in enumerate(column_constants(points)):
        for i, entry in enumerate(entries):
            tab_ref[j, i] = entry

    loads[0].wait()
    loads[1].wait()

    @pl.when(at_wall)
    def _():
        height = h[...]
        for c in range(2):
            picked = v[c, LEVELS]
            for level in range(1, LEVELS):
                picked = jnp.where(height == level, v[c, level], picked)
            for r in range(group):
                j, off = (r * block) // LANES, (r * block) % LANES
                part = picked[:, j * LANES : (j + 1) * LANES]
                if off:
                    part = pltpu.roll(part, LANES - off, 1)
                stage[r, c] = part
        sample_height = height.astype(jnp.float32) + 0.5
        for r in range(group):
            j, off = (r * block) // LANES, (r * block) % LANES
            part = sample_height[:, j * LANES : (j + 1) * LANES]
            if off:
                part = pltpu.roll(part, LANES - off, 1)
            stage[r, 2] = part
        tops[gy] = stage[me]

    @pl.when(first)
    def _():
        pl.semaphore_wait(barrier, group - 1)

    @pl.when(lead)
    def _():
        pl.semaphore_wait(ready, group - n_gz + 1)

    @pl.when(plain)
    def _():
        pl.semaphore_wait(barrier, group + 1)
        for side in (left, right):

            @pl.when((side == 0) | is_lead(side, gy, gz))
            def _():
                tell(ready, (side, gy, gz))

        for mate in mates:

            @pl.when(is_lead(*mate))
            def _():
                tell(ready, mate)

    def top_send(d):
        r = lax.rem(me + d, group)
        return pltpu.make_async_remote_copy(
            src_ref=stage.at[r], dst_ref=tops.at[gy], send_sem=t_send.at[d], recv_sem=t_recv.at[gy],
            device_id=(gx, r // n_gz, r % n_gz), device_id_type=MESH,
        )

    @pl.when(at_wall)
    def _():
        for d in range(1, group):
            top_send(d).start()

    @pl.when(lead)
    def _():
        for way, side in ((0, right), (1, left)):

            @pl.when(side != 0)
            def _():
                for k in range(CHUNKS):
                    x_copies(k)[way].start()

    @pl.when(plain)
    def _():
        for k in range(CHUNKS):
            for copy in x_copies(k):
                copy.start()

    edge = (layers - 1) * (1 - gz)
    z_copy = pltpu.make_async_remote_copy(
        src_ref=v_hbm.at[:, edge], dst_ref=zhalo, send_sem=z_send.at[0], recv_sem=z_recv.at[0],
        device_id=(gx, gy, 1 - gz), device_id_type=MESH,
    )
    z_copy.start()

    loads[2].wait()
    loads[3].wait()
    lane = lax.broadcasted_iota(jnp.int32, (rows, LANES), 1)

    def pack(k, carry):
        low, high = carry
        c, z = k // layers, k % layers
        low = jnp.where(lane == k, pltpu.roll(v[c, z, :, :LANES], k, 1), low)
        high = jnp.where(lane == k, pltpu.roll(v[c, z, :, width - LANES :], k + 1, 1), high)
        return low, high

    zeros = jnp.zeros((rows, LANES), jnp.float32)
    low, high = lax.fori_loop(0, 3 * layers, pack, (zeros, zeros), unroll=4)
    ypack_lo[...] = low
    ypack_hi[...] = high
    y_copies = [
        pltpu.make_async_remote_copy(
            src_ref=ypack_hi, dst_ref=ylo, send_sem=y_send.at[0], recv_sem=y_recv.at[0],
            device_id=(gx, above, gz), device_id_type=MESH,
        ),
        pltpu.make_async_remote_copy(
            src_ref=ypack_lo, dst_ref=yhi, send_sem=y_send.at[1], recv_sem=y_recv.at[1],
            device_id=(gx, below, gz), device_id_type=MESH,
        ),
    ]
    for copy in y_copies:
        copy.start()

    loads[4].wait()

    def shear(i, carry):
        du = s[0, i + 1] - s[0, i]
        dv = s[1, i + 1] - s[1, i]
        eddy[i] = tab_ref[1, i] * jnp.sqrt(du * du + dv * dv + 1e-06)
        return carry

    lax.fori_loop(0, points - 1, shear, 0, unroll=3)

    def top_wait(src):
        pltpu.make_async_remote_copy(
            src_ref=stage.at[0], dst_ref=tops.at[src], send_sem=t_send.at[0], recv_sem=t_recv.at[src],
            device_id=(gx, gy, 1 - gz), device_id_type=MESH,
        ).wait_recv()

    for src in range(n_gy):

        @pl.when(me != src * n_gz)
        def _():
            top_wait(src)

    def answer(now):
        @pl.when(first & now)
        def _():
            pl.semaphore_wait(ready, 2)
            for k in range(CHUNKS):
                for copy in x_copies(k):
                    copy.start()

    answer(gy == 0)
    halves = cols // LANES

    def interleave(field):
        parts = []
        for half in range(halves):
            source = (lane + half * LANES) // n_gy
            owner = (lane + half * LANES) % n_gy
            out = None
            for src in range(n_gy):
                got = jnp.take_along_axis(tops[src, field], source, axis=1, mode="promise_in_bounds")
                out = got if out is None else jnp.where(owner == src, got, out)
            parts.append(out)
        return jnp.concatenate(parts, axis=1)

    top_u, top_v, height = interleave(0), interleave(1), interleave(2)
    inv_height = 1.0 / height

    last = points - 1
    fresh_ref[0, last] = top_u
    fresh_ref[1, last] = top_v
    fresh_ref[0, 0] = jnp.zeros_like(top_u)
    fresh_ref[1, 0] = jnp.zeros_like(top_u)

    def eliminate(k, carry):
        share, cond, f_u, f_v = carry
        i = last - 1 - k
        cond_low = tab_ref[0, i - 1] * inv_height + eddy[i - 1]
        volume = tab_ref[2, i] * height
        held = volume + share
        inverse = 1.0 / (held + cond_low)
        f_u = (volume * s[0, i] + cond * f_u) * inverse
        f_v = (volume * s[1, i] + cond * f_v) * inverse
        coef_e[i] = cond_low * inverse
        coef_f[0, i] = f_u
        coef_f[1, i] = f_v
        return cond_low * (held * inverse), cond_low, f_u, f_v

    cond_top = tab_ref[0, last - 1] * inv_height + eddy[last - 1]
    _, cond, f_u, f_v = lax.fori_loop(0, points - 2, eliminate, (cond_top, cond_top, top_u, top_v), unroll=2)
    stress = (cond * f_u, cond * f_v)

    for src in range(n_gy):
        index = lane * n_gy + src
        index = jnp.where(index < cols, index, 0)
        for c in range(2):
            out = None
            for half in range(halves):
                got = jnp.take_along_axis(
                    stress[c][:, half * LANES : (half + 1) * LANES], index % LANES, axis=1, mode="promise_in_bounds"
                )
                out = got if out is None else jnp.where(index // LANES == half, got, out)
            back[src, c] = out

    def wall_send(src):
        return pltpu.make_async_remote_copy(
            src_ref=back.at[src], dst_ref=walls.at[me], send_sem=w_send.at[src], recv_sem=w_recv.at[me],
            device_id=(gx, src, 0), device_id_type=MESH,
        )

    for src in range(n_gy):

        @pl.when(me != src * n_gz)
        def _():
            wall_send(src).start()

    @pl.when(at_wall)
    def _():
        walls[me] = back[gy]

    answer(gy != 0)

    def substitute(k, carry):
        u, w = carry
        i = k + 1
        e = coef_e[i]
        u = e * u + coef_f[0, i]
        w = e * w + coef_f[1, i]
        fresh_ref[0, i] = u
        fresh_ref[1, i] = w
        return u, w

    zero = jnp.zeros_like(top_u)
    lax.fori_loop(0, points - 2, substitute, (zero, zero), unroll=2)

    for copy in y_copies:
        copy.wait_recv()
    z_copy.wait_recv()
    loads[5].wait()
    loads[6].wait()

    disks = mask[0]
    for k in range(1, 8):
        disks = jnp.maximum(disks, mask[k])
    force = jnp.zeros((rows, width), jnp.float32)
    for k in range(8):
        force = force + jnp.where(disks == k + 1, thrust_ref[k], 0.0)
    force = force * time_step
    for z in range(layers):
        if 2 <= z < 10:
            push[z] = jnp.where(jnp.logical_and(mask[z - 2] != 0, at_wall), force, 0.0)
        else:
            push[z] = jnp.zeros_like(force)

    row = lax.broadcasted_iota(jnp.int32, (rows, width), 0)
    col = lax.broadcasted_iota(jnp.int32, (rows, width), 1)

    def early(z, zp, zn):
        vel, yn, yp = [], [], []
        for c in range(3):
            here = v[c, z]
            vel.append(here)
            slot = c * layers + z
            low = pltpu.roll(ylo[...], LANES - slot, 1)
            high = pltpu.roll(yhi[...], LANES - 1 - slot, 1)
            low = jnp.concatenate([low] * tiles, axis=1)
            high = jnp.concatenate([high] * tiles, axis=1)
            yp.append(jnp.where(col == 0, low, pltpu.roll(here, 1, 1)))
            yn.append(jnp.where(col == width - 1, high, pltpu.roll(here, width - 1, 1)))
        d_y = [yn[c] - yp[c] for c in range(3)]
        d_z = [zn[c] - zp[c] for c in range(3)]
        s_yz = d_z[1] + d_y[2]
        part[0, z] = d_y[0]
        part[1, z] = d_z[0]
        part[2, z] = 0.5 * (d_y[1] * d_y[1] + d_z[2] * d_z[2]) + (0.25 * (s_yz * s_yz) + 1e-06)
        for c in range(3):
            part[3 + c, z] = (yn[c] + yp[c]) + (zn[c] + zp[c]) - 6.0 * vel[c]
            flux = (yn[c] * yn[1] - yp[c] * yp[1]) + (zn[c] * zn[2] - zp[c] * zp[2])
            kept = vel[c] - (0.5 * time_step) * flux
            part[6 + c, z] = kept - push[z] if c == 2 else kept

    def layer(z, wall):
        xn, xp = [], []
        for c in range(3):
            here = v[c, z]
            xp.append(jnp.where(row == 0, xlo[c, z], pltpu.roll(here, 1, 0)))
            xn.append(jnp.where(row == rows - 1, xhi[c, z], pltpu.roll(here, rows - 1, 0)))
        d_x = [xn[c] - xp[c] for c in range(3)]
        s_xy, s_xz = part[0, z] + d_x[1], part[1, z] + d_x[2]
        strain = jnp.sqrt(part[2, z] + (0.5 * (d_x[0] * d_x[0]) + 0.25 * (s_xy * s_xy + s_xz * s_xz)))
        viscous = time_step * viscosity + (time_step * smag_coeff) * strain
        for c in range(3):
            lap = part[3 + c, z] + (xn[c] + xp[c])
            if wall is not None and c < 2:
                lap = lap + v[c, z]
            out = part[6 + c, z] + (viscous * lap - (0.5 * time_step) * (xn[c] * xn[0] - xp[c] * xp[0]))
            if wall is not None and c < 2:
                out = out - time_step * wall[c]
            adv_ref[c, z] = out

    def velocity_at(z):
        return [v[c, z] for c in range(3)]

    bottom = at_wall.astype(jnp.float32)
    early(layers - 1, velocity_at(layers - 2), [zhalo[c] * bottom for c in range(3)])
    early(0, [zhalo[c] * (1.0 - bottom) for c in range(3)], velocity_at(1))

    def early_inner(z, carry):
        early(z, velocity_at(z - 1), velocity_at(z + 1))
        return carry

    lax.fori_loop(1, layers - 1, early_inner, 0)

    def x_wait(k):
        for copy in x_copies(k):
            copy.wait_recv()

    x_wait(0)
    layer(layers - 1, None)

    def inner(z, carry):
        layer(z, None)
        return carry

    lax.fori_loop(max(cuts[1], 1), layers - 1, inner, 0)
    for k in range(1, CHUNKS):
        x_wait(k)
        lax.fori_loop(max(cuts[k + 1], 1), cuts[k], inner, 0, unroll=2 if (cuts[k] - max(cuts[k + 1], 1)) % 2 == 0 else 1)

    def wall_wait(r):
        pltpu.make_async_remote_copy(
            src_ref=back.at[0], dst_ref=walls.at[r], send_sem=w_send.at[0], recv_sem=w_recv.at[r],
            device_id=(gx, gy, 1 - gz), device_id_type=MESH,
        ).wait_recv()

    @pl.when(at_wall)
    def _():
        for r in range(group):

            @pl.when(me != r)
            def _():
                wall_wait(r)

        wall = []
        for c in range(2):
            parts = []
            for j in range(tiles):
                out = None
                for r in range(group):
                    if (r * block) // LANES == j:
                        off = (r * block) % LANES
                        got = walls[r, c]
                        if off:
                            got = pltpu.roll(got, off, 1)
                        out = got if out is None else jnp.where(lane >= off, got, out)
                parts.append(out)
            wall.append(jnp.concatenate(parts, axis=1))
        layer(0, wall)

    @pl.when(jnp.logical_not(at_wall))
    def _():
        layer(0, None)

    @pl.when(at_wall)
    def _():
        for d in range(1, group):
            top_send(d).wait_send()

    for src in range(n_gy):

        @pl.when(me != src * n_gz)
        def _():
            wall_send(src).wait_send()

    for k in range(CHUNKS):
        for copy in x_copies(k):
            copy.wait_send()
    for copy in y_copies:
        copy.wait_send()
    z_copy.wait_send()


def write_out(advanced, fresh, advanced_hbm, fresh_hbm, sem):
    copies = [pltpu.make_async_copy(fresh.at[c], fresh_hbm.at[c], sem.at[c]) for c in range(2)]
    copies += [pltpu.make_async_copy(advanced.at[c], advanced_hbm.at[c], sem.at[2 + c]) for c in range(3)]
    for copy in copies:
        copy.start()
    for copy in copies:
        copy.wait()


def local(n_gx, n_gy, n_gz, velocity, column_state, height_index, rotor_mask, thrust):
    _, layers, rows, width = velocity.shape
    _, points, _, cols = column_state.shape
    group = n_gy * n_gz
    hbm_spec = pl.BlockSpec(memory_space=pltpu.HBM)
    vmem_spec = pl.BlockSpec(memory_space=pltpu.VMEM)
    f32 = jnp.float32
    dma = pltpu.SemaphoreType.DMA
    scratch = [
        pltpu.VMEM(velocity.shape, f32),
        pltpu.VMEM(column_state.shape, f32),
        pltpu.VMEM(height_index.shape, jnp.int32),
        pltpu.VMEM((8, rows, width), jnp.int32),
        pltpu.SMEM(thrust.shape, f32),
        pltpu.SMEM((3, points - 1), f32),
        pltpu.VMEM((points - 1, rows, cols), f32),
        pltpu.VMEM((points - 1, rows, cols), f32),
        pltpu.VMEM((2, points - 1, rows, cols), f32),
        pltpu.VMEM((3, layers, 1, width), f32),
        pltpu.VMEM((3, layers, 1, width), f32),
        pltpu.VMEM((3, rows, width), f32),
        pltpu.VMEM((rows, LANES), f32),
        pltpu.VMEM((rows, LANES), f32),
        pltpu.VMEM((rows, LANES), f32),
        pltpu.VMEM((rows, LANES), f32),
        pltpu.VMEM((group, 3, rows, LANES), f32),
        pltpu.VMEM((n_gy, 3, rows, LANES), f32),
        pltpu.VMEM((n_gy, 2, rows, LANES), f32),
        pltpu.VMEM((group, 2, rows, LANES), f32),
        pltpu.VMEM((layers, rows, width), f32),
        pltpu.VMEM((9, layers, rows, width), f32),
        dma((7,)),
        dma((2 * CHUNKS,)), dma((2 * CHUNKS,)),
        dma((2,)), dma((2,)),
        dma((1,)), dma((1,)),
        dma((group,)), dma((n_gy,)),
        dma((n_gy,)), dma((group,)),
        pltpu.SemaphoreType.REGULAR,
    ]
    sizes = (n_gx, n_gy, n_gz, layers, rows, width, points, cols)
    advanced, fresh = pl.pallas_call(
        functools.partial(kernel, sizes),
        out_shape=(
            jax.ShapeDtypeStruct(velocity.shape, f32),
            jax.ShapeDtypeStruct(column_state.shape, f32),
        ),
        in_specs=[hbm_spec] * 5,
        out_specs=(vmem_spec, vmem_spec),
        scratch_shapes=scratch,
        compiler_params=pltpu.CompilerParams(
            collective_id=0, has_side_effects=True, vmem_limit_bytes=32 * 1024 * 1024
        ),
    )(*[pltpu.with_memory_space_constraint(a, pltpu.HBM) for a in (velocity, column_state, height_index, rotor_mask, thrust)])

    return pl.pallas_call(
        write_out,
        out_shape=(
            jax.ShapeDtypeStruct(velocity.shape, f32),
            jax.ShapeDtypeStruct(column_state.shape, f32),
        ),
        in_specs=(vmem_spec, vmem_spec),
        out_specs=(hbm_spec, hbm_spec),
        scratch_shapes=[dma((5,))],
        compiler_params=pltpu.CompilerParams(vmem_limit_bytes=8 * 1024 * 1024),
    )(
        pltpu.with_memory_space_constraint(advanced, pltpu.VMEM),
        pltpu.with_memory_space_constraint(fresh, pltpu.VMEM),
    )


def solution(mesh):
    in_specs = (
        P(None, "gz", "gx", "gy"),
        P(None, None, "gx", ("gy", "gz")),
        P("gx", "gy"),
        P("gz", "gx", "gy"),
        P(),
    )
    out_specs = (P(None, "gz", "gx", "gy"), P(None, None, "gx", ("gy", "gz")))
    run = functools.partial(local, mesh.shape["gx"], mesh.shape["gy"], mesh.shape["gz"])
    return jax.shard_map(run, mesh=mesh, in_specs=in_specs, out_specs=out_specs, check_vma=False)
```
